32 devices in a mesh: groups: 2 (over y), tile: 4 (over z), slab: 4 (over x, core).
Axes of the slice: x: 2, y: 2, z: 4, core: 2. Of those that a mesh axis runs over, the one named last changes fastest.
Arguments:
- phase_map: float32 [32, 512, 512], P(('groups', 'slab'), 'tile'), parts along dimension 0, may hold values from -3 to 3
- absorption: float32 [32, 512, 512], P(('groups', 'slab'), 'tile'), parts along dimension 0, may hold values from 0 to 0.1
- probe_wave: float32 [2, 128, 128], replicated, may hold values from -6 to 6
- measured: float32 [32, 128, 128], P(('groups', 'tile')), parts along dimension 0, may hold values from 0 to 2
- rows_at: int32 [32], P(('groups', 'tile')), parts along dimension 0, may hold values from 0 to 127
- cols_at: int32 [32], P(('groups', 'tile')), parts along dimension 0, may hold values from 0 to 384
- live_mask: int32 [32], P(('groups', 'tile')), parts along dimension 0, may hold values 0 or 1
Outputs:
- grad_phase: float32 [32, 512, 512], P(('groups', 'slab'), 'tile'), parts along dimension 0
- grad_absorption: float32 [32, 512, 512], P(('groups', 'slab'), 'tile'), parts along dimension 0
The draws below stay inside these ranges and needn't reach their ends.
There are 2 independent parts, one for each index of `groups`. The reference program is written for one: setup_inputs(seed, part) draws one part's arguments, and reference() takes and returns one part's arrays. A program takes and returns all parts, laid end to end along the dimension named above; an argument that names none is the same for every part. Nothing has to cross between parts.
All inputs are finite; a program needn't handle non-finite values. No bound on the sum of `live_mask` on one device may be relied on, other than what follows from the above.
Results may differ from the reference program's by a relative error of at most 0.0003.
Values sent between devices are 32-bit elements; how exact they have to be, the bound alone decides.
A program may use at most 64 MiB of HBM per device.

```python
import math
import jax
import jax.numpy as jnp
from jax import lax

WIN = 128
COLS = 512
W_DEV = 4
ROWS_DEV = 128
SLICES = 16
ROWS = 512
WINDOWS = 16


def set_ends(drawn, key, low, high):
    spot = [jax.random.randint(jax.random.fold_in(key, axis), (), 0, length) for axis, length in enumerate(drawn.shape)]
    main_axis = drawn.shape.index(max(drawn.shape))
    next_to = spot[:main_axis] + [(spot[main_axis] + 1) % drawn.shape[main_axis]] + spot[main_axis + 1:]
    return drawn.at[tuple(spot)].set(low).at[tuple(next_to)].set(high)


def level_of(own_key, shape, cuts, low, top_value):
    factor_of, own = 1.0, jax.random.fold_in(own_key, 6)
    for dim, parts in cuts:
        steps = jnp.exp(jax.random.uniform(jax.random.fold_in(own, dim), (parts,), jnp.float32, low / len(cuts), top_value / len(cuts)))
        factor_of = factor_of * jnp.repeat(steps, shape[dim] // parts).reshape([-1 if axis == dim else 1 for axis in range(len(shape))])
    return factor_of


def normal_values(rng, shape, spread, most, split=(), held_as=jnp.bfloat16):
    array = spread * jax.random.normal(rng, shape, jnp.float32)
    if split:
        array = array * level_of(rng, shape, split, -0.22, 0.18)
    return jnp.clip(array, -most, most).astype(held_as)


def setup_inputs(seed: int = 0, part: int = 0) -> dict:
    splits = jax.random.split(jax.random.key(seed), 8)
    part_splits = jax.random.split(jax.random.fold_in(splits[7], part), 8)
    phase_map = normal_values(part_splits[0], (SLICES, ROWS, COLS), 0.5, 3.0, ((0, 4), (1, 4)), jnp.float32)
    absorption = jnp.clip(0.1 * jax.random.uniform(part_splits[1], (SLICES, ROWS, COLS), jnp.float32) ** level_of(part_splits[1], (SLICES, ROWS, COLS), ((0, 4), (1, 4)), -0.2, 0.2), 0.0, 0.1)
    probe_wave = normal_values(splits[2], (2, WIN, WIN), 1.0, 6.0, (), jnp.float32)
    measured = jnp.clip(2.0 * jax.random.uniform(part_splits[3], (WINDOWS, WIN, WIN), jnp.float32) ** level_of(part_splits[3], (WINDOWS, WIN, WIN), ((0, 4),), -0.2, 0.2), 0.0, 2.0)
    rows_at = set_ends(jax.random.randint(part_splits[4], (WINDOWS,), 0, ROWS_DEV), jax.random.fold_in(part_splits[4], 1), 0, ROWS_DEV - 1).astype(jnp.int32)
    cols_at = set_ends(jax.random.randint(part_splits[5], (WINDOWS,), 0, COLS - WIN + 1), jax.random.fold_in(part_splits[5], 1), 0, COLS - WIN).astype(jnp.int32)
    live_mask = set_ends((jax.random.randint(part_splits[6], (WINDOWS,), 0, 4) < 3).astype(jnp.int32), jax.random.fold_in(part_splits[6], 1), 0, 1)
    return {"phase_map": phase_map, "absorption": absorption, "probe_wave": probe_wave, "measured": measured, "rows_at": rows_at, "cols_at": cols_at, "live_mask": live_mask}


chirp_rate = 0.25
highest = lax.Precision.HIGHEST

def tables(length):
    index = jnp.arange(length, dtype=jnp.int32)
    signed = jnp.where(index < length // 2, index, index - length).astype(jnp.float32)
    chirped = -jnp.pi * chirp_rate * signed * signed / length
    product = index[:, None] * index[None, :] % length
    rotation = 2.0 * jnp.pi * product.astype(jnp.float32) / length
    angles = chirped[:, None] + rotation
    kernel_real = lax.optimization_barrier(jnp.sum(jnp.cos(angles), axis=0)) / length
    kernel_imag = lax.optimization_barrier(jnp.sum(jnp.sin(angles), axis=0)) / length
    lagged = (index[:, None] - index[None, :]) % length
    norm_scale = 1.0 / math.sqrt(length)
    return (kernel_real[lagged], kernel_imag[lagged], jnp.cos(rotation) * norm_scale, -jnp.sin(rotation) * norm_scale)

def sandwich(mat_real, mat_imag, wave_real, wave_imag, conj_sign):
    mat_other = conj_sign * mat_imag
    left_real = jnp.einsum('ij,bjk->bik', mat_real, wave_real, precision=highest) - jnp.einsum('ij,bjk->bik', mat_other, wave_imag, precision=highest)
    left_imag = jnp.einsum('ij,bjk->bik', mat_real, wave_imag, precision=highest) + jnp.einsum('ij,bjk->bik', mat_other, wave_real, precision=highest)
    out_real = jnp.einsum('bij,jk->bik', left_real, mat_real, precision=highest) - jnp.einsum('bij,jk->bik', left_imag, mat_other, precision=highest)
    out_imag = jnp.einsum('bij,jk->bik', left_real, mat_other, precision=highest) + jnp.einsum('bij,jk->bik', left_imag, mat_real, precision=highest)
    return (out_real, out_imag)

def window_loss(patch_phase, patch_absorb, probe_wave, measured_one, weight_one, matrices):
    spread_real, spread_imag, fourier_real, fourier_imag = matrices
    wave_real = probe_wave[0][None]
    wave_imag = probe_wave[1][None]
    for layer_index in range(patch_phase.shape[0]):
        damping = jnp.exp(-patch_absorb[layer_index])[None]
        trans_real = damping * jnp.cos(patch_phase[layer_index])[None]
        trans_imag = damping * jnp.sin(patch_phase[layer_index])[None]
        mixed_real = trans_real * wave_real - trans_imag * wave_imag
        mixed_imag = trans_real * wave_imag + trans_imag * wave_real
        wave_real, wave_imag = sandwich(spread_real, spread_imag, mixed_real, mixed_imag, 1.0)
    far_real, far_imag = sandwich(fourier_real, fourier_imag, wave_real, wave_imag, 1.0)
    excess = far_real * far_real + far_imag * far_imag - measured_one[None]
    return 0.125 * weight_one * jnp.sum(excess * excess)

def reference(phase_map, absorption, probe_wave, measured, rows_at, cols_at, live_mask):
    matrices = tables(WIN)
    padding = jnp.zeros((SLICES, WIN, COLS), phase_map.dtype)
    phase_pad = jnp.concatenate([phase_map, padding], axis=1)
    absorb_pad = jnp.concatenate([absorption, padding], axis=1)
    anchor = jnp.zeros((), jnp.int32)

    def visit(carried, slot):
        grad_phase_pad, grad_absorb_pad = carried
        tile_index = (slot // W_DEV).astype(jnp.int32)
        top_row = (tile_index * ROWS_DEV + rows_at[slot]).astype(jnp.int32)
        left_col = cols_at[slot].astype(jnp.int32)
        corner = (anchor, top_row, left_col)
        extent = (SLICES, WIN, WIN)
        patch_phase = lax.dynamic_slice(phase_pad, corner, extent)
        patch_absorb = lax.dynamic_slice(absorb_pad, corner, extent)
        weight_one = live_mask[slot].astype(phase_map.dtype)

        def loss_of(first_arg, second_arg):
            return window_loss(first_arg, second_arg, probe_wave, measured[slot], weight_one, matrices)
        unused, pullback = jax.vjp(loss_of, patch_phase, patch_absorb)
        d_phase, d_absorb = pullback(jnp.ones((), phase_map.dtype))
        grad_phase_pad = lax.dynamic_update_slice(grad_phase_pad, lax.dynamic_slice(grad_phase_pad, corner, extent) + d_phase, corner)
        grad_absorb_pad = lax.dynamic_update_slice(grad_absorb_pad, lax.dynamic_slice(grad_absorb_pad, corner, extent) + d_absorb, corner)
        return ((grad_phase_pad, grad_absorb_pad), None)
    start = (jnp.zeros_like(phase_pad), jnp.zeros_like(absorb_pad))
    totals, unused_out = lax.scan(visit, start, jnp.arange(WINDOWS, dtype=jnp.int32))
    return (totals[0][:, :ROWS, :], totals[1][:, :ROWS, :])
```

```python
import functools
import math

import jax
import jax.numpy as jnp
import ml_dtypes
import numpy as np
from jax import lax
from jax.experimental import pallas as pl
from jax.experimental.pallas import tpu as pltpu
from jax.sharding import PartitionSpec as P

chirp_rate = 0.25
vmem_limit = 56 * 1024 * 1024


def split_host(mat):
    high = mat.astype(np.float32).astype(ml_dtypes.bfloat16)
    low = (mat - high.astype(np.float64)).astype(np.float32).astype(ml_dtypes.bfloat16)
    return high, low


def tables(length):
    index = np.arange(length)
    signed = np.where(index < length // 2, index, index - length).astype(np.float64)
    chirped = -np.pi * chirp_rate * signed * signed / length
    rotation = 2.0 * np.pi * (index[:, None] * index[None, :] % length) / length
    kernel = np.exp(1j * (chirped[:, None] + rotation)).sum(axis=0) / length
    spread = kernel[(index[:, None] - index[None, :]) % length]
    fourier = np.exp(-1j * rotation) / math.sqrt(length)
    forms = []
    for mat in (spread, fourier):
        re, im = mat.real, mat.imag
        minus = np.block([[re, im], [-im, re]])
        plus = np.block([[re, -im], [im, re]])
        for block in (minus, plus):
            high, low = split_host(block)
            forms.append(
                (np.concatenate([high, high, low], axis=0), np.concatenate([high, high, low], axis=1))
            )
    (q_minus, q_plus, f_minus, f_plus) = forms
    return (
        q_plus[1], q_minus[0], q_minus[1], q_plus[0],
        f_plus[1], f_minus[0], f_minus[1], f_plus[0],
    )


def halves(array):
    high = array.astype(jnp.bfloat16)
    low = (array - high.astype(jnp.float32)).astype(jnp.bfloat16)
    return high, low


def sandwich(left_ref, right_ref, wave_real, wave_imag):
    side = wave_real.shape[0]
    high, low = halves(jnp.concatenate([wave_real, wave_imag], axis=1))
    beside = jnp.dot(
        jnp.concatenate([high, low, high], axis=1), right_ref[...],
        preferred_element_type=jnp.float32,
    )
    high, low = halves(jnp.concatenate([beside[:, :side], beside[:, side:]], axis=0))
    stacked = jnp.dot(
        left_ref[...], jnp.concatenate([high, low, high], axis=0),
        preferred_element_type=jnp.float32,
    )
    return stacked[:side], stacked[side:]


def cos_sin(angle):
    turns = jnp.floor(angle * (2.0 / math.pi) + 0.5)
    rest = angle - turns * 1.5703125
    rest = rest - turns * 4.837512969970703e-4
    rest = rest - turns * 7.549789948768648e-8
    sq = rest * rest
    sin_part = rest + rest * sq * (-1.6666654611e-1 + sq * (8.3321608736e-3 + sq * -1.9515295891e-4))
    cos_part = 1.0 - 0.5 * sq + sq * sq * (
        4.166664568298827e-2 + sq * (-1.388731625493765e-3 + sq * 2.443315711809948e-5)
    )
    half = jnp.floor(turns * 0.5)
    odd = (turns - 2.0 * half) > 0.5
    flip = 1.0 - 2.0 * (half - 2.0 * jnp.floor(half * 0.5))
    cos_out = jnp.where(odd, -sin_part, cos_part) * flip
    sin_out = jnp.where(odd, cos_part, sin_part) * flip
    return cos_out, sin_out


def column_base(col, side, cols):
    return pl.multiple_of(jnp.minimum(col // side, cols // side - 2) * side, side)


def cut_kernel(rows_ref, cols_ref, phase_ref, absorb_ref, below_phase_ref, below_absorb_ref, out_ref, tall):
    window, layers, _, side, _ = out_ref.shape
    cols = phase_ref.shape[2]
    for layer in range(layers):
        for which, (upper, lower) in enumerate(
            ((phase_ref, below_phase_ref), (absorb_ref, below_absorb_ref))
        ):
            tall[layer, which, :side] = upper[layer]
            tall[layer, which, side:] = lower[layer]

    def one(w, carried):
        row, col = rows_ref[w], cols_ref[w]
        base = column_base(col, side, cols)
        shift = lax.rem(2 * side - (col - base), 2 * side)
        top = pl.multiple_of(row // 8 * 8, 8)
        lift = lax.rem(side + 8 - (row - top), side + 8)
        for layer in range(layers):
            for which in range(2):
                wide = tall[layer, which, pl.ds(top, side + 8), pl.ds(base, 2 * side)]
                narrow = pltpu.roll(wide, shift, 1)[:, :side]
                out_ref[w, layer, which] = pltpu.roll(narrow, lift, 0)[:side]
        return carried

    lax.fori_loop(0, rows_ref.shape[0], one, 0)


def place_kernel(rows_ref, cols_ref, pieces_ref, own_phase, own_absorb, spill_ref, tall):
    _, layers, _, side, _ = pieces_ref.shape
    cols = own_phase.shape[2]
    tall[...] = jnp.zeros_like(tall)

    def one(w, carried):
        row, col = rows_ref[w], cols_ref[w]
        base = column_base(col, side, cols)
        shift = col - base
        top = pl.multiple_of(row // 8 * 8, 8)
        for layer in range(layers):
            for which in range(2):
                piece = pieces_ref[w, layer, which]
                long = pltpu.roll(jnp.concatenate([piece, jnp.zeros_like(piece[:8])], axis=0), row - top, 0)
                wide = pltpu.roll(jnp.concatenate([long, jnp.zeros_like(long)], axis=1), shift, 1)
                where = (layer, which, pl.ds(top, side + 8), pl.ds(base, 2 * side))
                tall[where] = tall[where] + wide
        return carried

    lax.fori_loop(0, rows_ref.shape[0], one, 0)
    for layer in range(layers):
        own_phase[layer] = tall[layer, 0, :side]
        own_absorb[layer] = tall[layer, 1, :side]
        for which in range(2):
            spill_ref[which, layer] = tall[layer, which, side:]


def wave_kernel(
    place_ref, live_ref, patches, probe_ref, measured_ref,
    q_left, q_right, qa_left, qa_right, f_left, f_right, fa_left, fa_right,
    grads, trans, mixed,
):
    slabs, _, layers, _, side, _ = patches.shape
    total = slabs * layers

    def prepare(s, carried):
        slab, layer = s // layers, lax.rem(s, layers)
        damping = jnp.exp(-patches[slab, 0, layer, 1])
        cos_part, sin_part = cos_sin(patches[slab, 0, layer, 0])
        trans[s, 0] = damping * cos_part
        trans[s, 1] = damping * sin_part
        return carried

    lax.fori_loop(0, total, prepare, 0)

    def forward(s, wave):
        wave_real, wave_imag = wave
        t_real, t_imag = trans[s, 0], trans[s, 1]
        mixed_real = t_real * wave_real - t_imag * wave_imag
        mixed_imag = t_real * wave_imag + t_imag * wave_real
        mixed[s, 0] = mixed_real
        mixed[s, 1] = mixed_imag
        return sandwich(q_left, q_right, mixed_real, mixed_imag)

    wave = lax.fori_loop(0, total, forward, (probe_ref[0], probe_ref[1]))
    far_real, far_imag = sandwich(f_left, f_right, *wave)
    slot = place_ref[0] * pl.num_programs(0) + pl.program_id(0)
    held = place_ref[1]
    weight = jnp.where(slot < held, live_ref[jnp.minimum(slot, held - 1)], 0).astype(jnp.float32)
    excess = (0.5 * weight) * (far_real * far_real + far_imag * far_imag - measured_ref[0])
    back = sandwich(fa_left, fa_right, excess * far_real, excess * far_imag)

    def backward(i, back):
        s = total - 1 - i
        slab, layer = s // layers, lax.rem(s, layers)
        m_real, m_imag = sandwich(qa_left, qa_right, *back)
        u_real, u_imag = mixed[s, 0], mixed[s, 1]
        t_real, t_imag = trans[s, 0], trans[s, 1]
        grads[slab, 0, layer, 0] = u_real * m_imag - u_imag * m_real
        grads[slab, 0, layer, 1] = -(u_real * m_real + u_imag * m_imag)
        return t_real * m_real + t_imag * m_imag, t_real * m_imag - t_imag * m_real

    lax.fori_loop(0, total, backward, back)


def passed_along(array, axis, by):
    devices = lax.axis_size(axis)
    pairs = [(i, i + by) for i in range(devices) if 0 <= i + by < devices]
    return lax.ppermute(array, axis, pairs)


def params():
    return pltpu.CompilerParams(vmem_limit_bytes=vmem_limit)


def local(phase_map, absorption, probe_wave, measured, rows_at, cols_at, live_mask):
    layers, rows, cols = phase_map.shape
    side = probe_wave.shape[2]
    windows = measured.shape[0]
    slabs = lax.axis_size("slab")
    per_slab = -(-windows // slabs)
    slots = per_slab * slabs
    smem = pl.BlockSpec(memory_space=pltpu.SMEM)
    vmem = pl.BlockSpec(memory_space=pltpu.VMEM)
    f32 = jnp.float32

    below_phase, below_absorb = passed_along((phase_map, absorption), "tile", -1)
    patches = pl.pallas_call(
        cut_kernel,
        out_shape=jax.ShapeDtypeStruct((slots, layers, 2, side, side), f32),
        in_specs=[smem, smem, vmem, vmem, vmem, vmem],
        out_specs=vmem,
        scratch_shapes=[pltpu.VMEM((layers, 2, 2 * side, cols), f32)],
        compiler_params=params(),
        name="cut",
    )(rows_at, cols_at, phase_map, absorption, below_phase, below_absorb)
    patches = patches.reshape(slabs, per_slab, layers, 2, side, side)
    patches = lax.all_to_all(patches, "slab", 0, 0, tiled=True)

    place = jnp.stack([lax.axis_index("slab"), jnp.int32(windows)]).astype(jnp.int32)
    mats = [jnp.asarray(m) for m in tables(side)]
    block = (slabs, 1, layers, 2, side, side)
    whole = lambda m: pl.BlockSpec(m.shape, lambda g, *_: (0,) * m.ndim)
    grads = pl.pallas_call(
        wave_kernel,
        out_shape=jax.ShapeDtypeStruct(patches.shape, f32),
        grid_spec=pltpu.PrefetchScalarGridSpec(
            num_scalar_prefetch=2,
            grid=(per_slab,),
            in_specs=[
                pl.BlockSpec(block, lambda g, *_: (0, g, 0, 0, 0, 0)),
                whole(probe_wave),
                pl.BlockSpec(
                    (1, side, side),
                    lambda g, place, live: (jnp.minimum(place[0] * per_slab + g, windows - 1), 0, 0),
                ),
            ] + [whole(m) for m in mats],
            out_specs=pl.BlockSpec(block, lambda g, *_: (0, g, 0, 0, 0, 0)),
            scratch_shapes=[
                pltpu.VMEM((slabs * layers, 2, side, side), f32),
                pltpu.VMEM((slabs * layers, 2, side, side), f32),
            ],
        ),
        compiler_params=params(),
        name="waves",
    )(place, live_mask, patches, probe_wave, measured, *mats)

    grads = lax.all_to_all(grads, "slab", 0, 0, tiled=True)
    grads = grads.reshape(slots, layers, 2, side, side)
    own_phase, own_absorb, spill = pl.pallas_call(
        place_kernel,
        out_shape=(
            jax.ShapeDtypeStruct(phase_map.shape, f32),
            jax.ShapeDtypeStruct(phase_map.shape, f32),
            jax.ShapeDtypeStruct((2,) + phase_map.shape, f32),
        ),
        in_specs=[smem, smem, vmem],
        out_specs=(vmem, vmem, vmem),
        scratch_shapes=[pltpu.VMEM((layers, 2, 2 * side, cols), f32)],
        compiler_params=params(),
        name="place",
    )(rows_at, cols_at, grads)
    from_above = passed_along(spill, "tile", 1)
    return own_phase + from_above[0], own_absorb + from_above[1]


def solution(mesh):
    return jax.shard_map(
        local,
        mesh=mesh,
        in_specs=(
            P(("groups", "slab"), "tile", None),
            P(("groups", "slab"), "tile", None),
            P(),
            P(("groups", "tile"), None, None),
            P(("groups", "tile")),
            P(("groups", "tile")),
            P(("groups", "tile")),
        ),
        out_specs=(P(("groups", "slab"), "tile", None), P(("groups", "slab"), "tile", None)),
        check_vma=False,
    )
```

```python
import functools
import math

import jax
import jax.numpy as jnp
import ml_dtypes
import numpy as np
from jax import lax
from jax.experimental import pallas as pl
from jax.experimental.pallas import tpu as pltpu
from jax.sharding import PartitionSpec as P

chirp_rate = 0.25
MESH = pl.DeviceIdType.MESH
vmem_limit = 56 * 1024 * 1024


def split_host(mat):
    high = mat.astype(np.float32).astype(ml_dtypes.bfloat16)
    low = (mat - high.astype(np.float64)).astype(np.float32).astype(ml_dtypes.bfloat16)
    return high, low


def tables(length):
    index = np.arange(length)
    signed = np.where(index < length // 2, index, index - length).astype(np.float64)
    chirped = -np.pi * chirp_rate * signed * signed / length
    rotation = 2.0 * np.pi * (index[:, None] * index[None, :] % length) / length
    kernel = np.exp(1j * (chirped[:, None] + rotation)).sum(axis=0) / length
    spread = kernel[(index[:, None] - index[None, :]) % length]
    fourier = np.exp(-1j * rotation) / math.sqrt(length)
    forms = []
    for mat in (spread, fourier):
        re, im = mat.real, mat.imag
        minus = np.block([[re, im], [-im, re]])
        plus = np.block([[re, -im], [im, re]])
        for block in (minus, plus):
            high, low = split_host(block)
            forms.append(
                (np.concatenate([high, high, low], axis=0), np.concatenate([high, high, low], axis=1))
            )
    (q_minus, q_plus, f_minus, f_plus) = forms
    return (
        q_plus[1], q_minus[0], q_minus[1], q_plus[0],
        f_plus[1], f_minus[0], f_minus[1], f_plus[0],
    )


def halves(array):
    high = array.astype(jnp.bfloat16)
    low = (array - high.astype(jnp.float32)).astype(jnp.bfloat16)
    return high, low


def sandwich(left_ref, right_ref, wave_real, wave_imag):
    side = wave_real.shape[0]
    high, low = halves(jnp.concatenate([wave_real, wave_imag], axis=1))
    beside = jnp.dot(
        jnp.concatenate([high, low, high], axis=1), right_ref[...],
        preferred_element_type=jnp.float32,
    )
    high, low = halves(jnp.concatenate([beside[:, :side], beside[:, side:]], axis=0))
    stacked = jnp.dot(
        left_ref[...], jnp.concatenate([high, low, high], axis=0),
        preferred_element_type=jnp.float32,
    )
    return stacked[:side], stacked[side:]


def cos_sin(angle):
    turns = jnp.floor(angle * (2.0 / math.pi) + 0.5)
    rest = angle - turns * 1.5703125
    rest = rest - turns * 4.837512969970703e-4
    rest = rest - turns * 7.549789948768648e-8
    sq = rest * rest
    sin_part = rest + rest * sq * (-1.6666654611e-1 + sq * (8.3321608736e-3 + sq * -1.9515295891e-4))
    cos_part = 1.0 - 0.5 * sq + sq * sq * (
        4.166664568298827e-2 + sq * (-1.388731625493765e-3 + sq * 2.443315711809948e-5)
    )
    half = jnp.floor(turns * 0.5)
    odd = (turns - 2.0 * half) > 0.5
    flip = 1.0 - 2.0 * (half - 2.0 * jnp.floor(half * 0.5))
    cos_out = jnp.where(odd, -sin_part, cos_part) * flip
    sin_out = jnp.where(odd, cos_part, sin_part) * flip
    return cos_out, sin_out


def column_base(col, side, cols):
    return pl.multiple_of(jnp.minimum(col // side, cols // side - 2) * side, side)


def cut_kernel(own_ref, above_ref, phase_ref, absorb_ref, own_out, above_out, tall):
    windows, layers, _, side, _ = own_out.shape
    cols = phase_ref.shape[2]
    for layer in range(layers):
        for which, source in enumerate((phase_ref, absorb_ref)):
            blank = jnp.zeros((side, cols), jnp.float32)
            tall[layer, which, :side] = blank
            tall[layer, which, side : 2 * side] = source[layer]
            tall[layer, which, 2 * side :] = blank

    def one(w, carried):
        for index_ref, out_ref, start in ((own_ref, own_out, side), (above_ref, above_out, 0)):
            row, col = index_ref[w], index_ref[windows + w]
            base = column_base(col, side, cols)
            shift = lax.rem(2 * side - (col - base), 2 * side)
            top = pl.multiple_of(row // 8 * 8, 8)
            lift = lax.rem(side + 8 - (row - top), side + 8)
            for layer in range(layers):
                for which in range(2):
                    wide = tall[layer, which, pl.ds(start + top, side + 8), pl.ds(base, 2 * side)]
                    narrow = pltpu.roll(wide, shift, 1)[:, :side]
                    out_ref[w, layer, which] = pltpu.roll(narrow, lift, 0)[:side]
        return carried

    lax.fori_loop(0, windows, one, 0)


def place_kernel(own_ref, above_ref, own_pieces, above_pieces, out_phase, out_absorb, tall):
    windows, layers, _, side, _ = own_pieces.shape
    cols = out_phase.shape[2]
    tall[...] = jnp.zeros_like(tall)

    def place(index_ref, pieces_ref, start, w):
        row, col = index_ref[w], index_ref[windows + w]
        base = column_base(col, side, cols)
        shift = col - base
        top = pl.multiple_of(row // 8 * 8, 8)
        for layer in range(layers):
            for which in range(2):
                piece = pieces_ref[w, layer, which]
                long = pltpu.roll(jnp.concatenate([piece, jnp.zeros_like(piece[:8])], axis=0), row - top, 0)
                wide = pltpu.roll(jnp.concatenate([long, jnp.zeros_like(long)], axis=1), shift, 1)
                where = (layer, which, pl.ds(start + top, side + 8), pl.ds(base, 2 * side))
                tall[where] = tall[where] + wide

    @pl.loop(0, windows)
    def _(w):
        place(own_ref, own_pieces, side, w)

        @pl.when(lax.axis_index("tile") > 0)
        def _():
            place(above_ref, above_pieces, 0, w)

    for layer in range(layers):
        out_phase[layer] = tall[layer, 0, side : 2 * side]
        out_absorb[layer] = tall[layer, 1, side : 2 * side]


def greet():
    slab, slabs = lax.axis_index("slab"), lax.axis_size("slab")
    tile, tiles = lax.axis_index("tile"), lax.axis_size("tile")
    barrier = pltpu.get_barrier_semaphore()
    for step in range(1, slabs):
        pl.semaphore_signal(
            barrier, inc=1, device_id={"slab": lax.rem(slab + step, slabs)}, device_id_type=MESH
        )

    @pl.when(tile > 0)
    def _():
        pl.semaphore_signal(barrier, inc=1, device_id={"tile": tile - 1}, device_id_type=MESH)

    @pl.when(tile < tiles - 1)
    def _():
        pl.semaphore_signal(barrier, inc=1, device_id={"tile": tile + 1}, device_id_type=MESH)

    beside = (tile > 0).astype(jnp.int32) + (tile < tiles - 1).astype(jnp.int32)
    pl.semaphore_wait(barrier, slabs - 1 + beside)


def slot_plan(windows, slabs):
    moved = windows // 2
    kept = windows - moved
    return kept, moved, -(-(windows + moved) // slabs)


def gather_kernel(own, above, patches, from_below, from_above, merged, zs_sem, zr_sem, xs_sem, xr_sem):
    windows, layers = own.shape[:2]
    slab, slabs = lax.axis_index("slab"), lax.axis_size("slab")
    tile, tiles = lax.axis_index("tile"), lax.axis_size("tile")
    kept, moved, _ = slot_plan(windows, slabs)
    first, last = tile == 0, tile == tiles - 1
    greet()

    def up(i, l):
        return pltpu.make_async_remote_copy(
            src_ref=above.at[i, l], dst_ref=from_below.at[i, l], send_sem=zs_sem.at[i, l],
            recv_sem=zr_sem.at[i, l], device_id={"tile": tile - 1}, device_id_type=MESH)

    def down(j, l):
        return pltpu.make_async_remote_copy(
            src_ref=own.at[kept + j, l], dst_ref=from_above.at[j, l], send_sem=zs_sem.at[kept + j, l],
            recv_sem=zr_sem.at[kept + j, l], device_id={"tile": tile + 1}, device_id_type=MESH)

    def across(k, source, l, sender):
        return pltpu.make_async_remote_copy(
            src_ref=source, dst_ref=patches.at[k // slabs, sender * layers + l], send_sem=xs_sem.at[k, l],
            recv_sem=xr_sem.at[k // slabs, sender, l], device_id={"slab": k % slabs}, device_id_type=MESH)

    @pl.loop(0, layers)
    def _(l):
        @pl.when(jnp.logical_not(first))
        def _():
            for i in range(kept):
                up(i, l).start()

        @pl.when(jnp.logical_not(last))
        def _():
            for j in range(moved):
                down(j, l).start()

    def hand_over(k, source, l):
        @pl.when(slab != k % slabs)
        def _():
            across(k, source, l, slab).start()

        @pl.when(slab == k % slabs)
        def _():
            patches[k // slabs, slab * layers + l] = source[...]

    @pl.when(last)
    def _():
        @pl.loop(0, layers)
        def _(l):
            for j in range(moved):
                hand_over(windows + j, own.at[kept + j, l], l)

    @pl.loop(0, layers)
    def _(l):
        for i in range(kept):
            @pl.when(last)
            def _():
                merged[i, l] = own[i, l]

            @pl.when(jnp.logical_not(last))
            def _():
                up(i, l).wait_recv()
                merged[i, l] = own[i, l] + from_below[i, l]

            hand_over(i, merged.at[i, l], l)

        @pl.when(jnp.logical_not(first))
        def _():
            for j in range(moved):
                down(j, l).wait_recv()
                merged[kept + j, l] = above[kept + j, l] + from_above[j, l]
                hand_over(kept + j, merged.at[kept + j, l], l)

    def finish(k, source):
        @pl.when(slab != k % slabs)
        def _():
            @pl.loop(0, layers)
            def _(l):
                across(k, source.at[l], l, slab).wait_send()

        @pl.when(slab == k % slabs)
        def _():
            for sender in range(slabs):
                @pl.when(sender != slab)
                def _():
                    @pl.loop(0, layers)
                    def _(l):
                        across(k, source.at[l], l, sender).wait_recv()

    for i in range(kept):
        finish(i, merged.at[i])

    @pl.when(jnp.logical_not(first))
    def _():
        for j in range(moved):
            finish(kept + j, merged.at[kept + j])

        @pl.loop(0, layers)
        def _(l):
            for i in range(kept):
                up(i, l).wait_send()

    @pl.when(last)
    def _():
        for j in range(moved):
            finish(windows + j, own.at[kept + j])

    @pl.when(jnp.logical_not(last))
    def _():
        @pl.loop(0, layers)
        def _(l):
            for j in range(moved):
                down(j, l).wait_send()


def scatter_kernel(grads, own, above, zs_sem, xs_sem, own_sem, above_sem):
    windows, layers = own.shape[:2]
    slab, slabs = lax.axis_index("slab"), lax.axis_size("slab")
    tile, tiles = lax.axis_index("tile"), lax.axis_size("tile")
    kept, moved, _ = slot_plan(windows, slabs)
    first, last = tile == 0, tile == tiles - 1
    greet()

    def home(k, l):
        if k < kept:
            return own.at[k, l], own_sem.at[k, l]
        if k < windows:
            return above.at[k, l], above_sem.at[k, l]
        return own.at[k - moved, l], own_sem.at[k - moved, l]

    def across(k, l, target):
        place, sem = home(k, l)
        return pltpu.make_async_remote_copy(
            src_ref=grads.at[k // slabs, target * layers + l], dst_ref=place,
            send_sem=xs_sem.at[k // slabs, target, l], recv_sem=sem,
            device_id={"slab": target}, device_id_type=MESH)

    def down(i, l):
        return pltpu.make_async_remote_copy(
            src_ref=own.at[i, l], dst_ref=above.at[i, l], send_sem=zs_sem.at[i, l],
            recv_sem=above_sem.at[i, l], device_id={"tile": tile + 1}, device_id_type=MESH)

    def up(k, l):
        return pltpu.make_async_remote_copy(
            src_ref=above.at[k, l], dst_ref=own.at[k, l], send_sem=zs_sem.at[k, l],
            recv_sem=own_sem.at[k, l], device_id={"tile": tile - 1}, device_id_type=MESH)

    def give(k, l):
        @pl.when(slab == k % slabs)
        def _():
            for target in range(slabs):
                @pl.when(slab != target)
                def _():
                    across(k, l, target).start()

            home(k, l)[0][...] = grads[k // slabs, slab * layers + l]

    @pl.loop(0, layers)
    def _(l):
        for k in range(kept):
            give(k, l)

        @pl.when(jnp.logical_not(first))
        def _():
            for k in range(kept, windows):
                give(k, l)

        @pl.when(last)
        def _():
            for k in range(windows, windows + moved):
                give(k, l)

    def arrive(k, l):
        @pl.when(slab != k % slabs)
        def _():
            across(k, l, slab).wait_recv()

    @pl.loop(0, layers)
    def _(l):
        for k in range(kept):
            arrive(k, l)

            @pl.when(jnp.logical_not(last))
            def _():
                down(k, l).start()

        @pl.when(jnp.logical_not(first))
        def _():
            for k in range(kept, windows):
                arrive(k, l)
                up(k, l).start()

    def sent(k, l):
        @pl.when(slab == k % slabs)
        def _():
            for target in range(slabs):
                @pl.when(slab != target)
                def _():
                    across(k, l, target).wait_send()

    @pl.loop(0, layers)
    def _(l):
        for k in range(kept):
            sent(k, l)

        @pl.when(jnp.logical_not(first))
        def _():
            for k in range(kept, windows):
                sent(k, l)
                up(k, l).wait_send()
            for k in range(kept):
                down(k, l).wait_recv()

        @pl.when(jnp.logical_not(last))
        def _():
            for k in range(kept):
                down(k, l).wait_send()
            for k in range(kept, windows):
                up(k, l).wait_recv()

        @pl.when(last)
        def _():
            for k in range(windows, windows + moved):
                arrive(k, l)
                sent(k, l)


def wave_kernel(
    own_ref, above_ref, patches, probe_ref, measured_ref, above_measured_ref,
    q_left, q_right, qa_left, qa_right, f_left, f_right, fa_left, fa_right,
    grads, trans, mixed,
):
    depth, total, _, side, _ = patches.shape
    windows = measured_ref.shape[0]
    slab, slabs = lax.axis_index("slab"), lax.axis_size("slab")
    tile, tiles = lax.axis_index("tile"), lax.axis_size("tile")
    kept, moved, _ = slot_plan(windows, slabs)

    def valid(d):
        k = d * slabs + slab
        mine = k < kept
        from_above = (k >= kept) & (k < windows) & (tile > 0)
        extra = (k >= windows) & (k < windows + moved) & (tile == tiles - 1)
        return mine | from_above | extra

    def far_side(d, wave):
        k = d * slabs + slab
        is_above = (k >= kept) & (k < windows)
        own_at = jnp.clip(jnp.where(k < windows, k, k - moved), 0, windows - 1)
        above_at = jnp.clip(k, kept, windows - 1)
        live = jnp.where(is_above, above_ref[2 * windows + above_at], own_ref[2 * windows + own_at])
        target = jnp.where(is_above, above_measured_ref[above_at - kept], measured_ref[own_at])
        far_real, far_imag = sandwich(f_left, f_right, *wave)
        excess = (0.5 * live.astype(jnp.float32)) * (far_real * far_real + far_imag * far_imag - target)
        return sandwich(fa_left, fa_right, excess * far_real, excess * far_imag)

    def run(slots):
        def prepare(s, carried):
            for d in slots:
                damping = jnp.exp(-patches[d, s, 1])
                cos_part, sin_part = cos_sin(patches[d, s, 0])
                trans[d, s, 0] = damping * cos_part
                trans[d, s, 1] = damping * sin_part
            return carried

        lax.fori_loop(0, total, prepare, 0)

        def forward(s, waves):
            entering = []
            for d, (wave_real, wave_imag) in zip(slots, waves):
                t_real, t_imag = trans[d, s, 0], trans[d, s, 1]
                mixed_real = t_real * wave_real - t_imag * wave_imag
                mixed_imag = t_real * wave_imag + t_imag * wave_real
                mixed[d, s, 0] = mixed_real
                mixed[d, s, 1] = mixed_imag
                entering.append((mixed_real, mixed_imag))
            return tuple(sandwich(q_left, q_right, *wave) for wave in entering)

        waves = lax.fori_loop(0, total, forward, tuple((probe_ref[0], probe_ref[1]) for d in slots))
        backs = tuple(far_side(d, wave) for d, wave in zip(slots, waves))

        def backward(i, backs):
            s = total - 1 - i
            result = []
            for d, (m_real, m_imag) in zip(slots, [sandwich(qa_left, qa_right, *back) for back in backs]):
                u_real, u_imag = mixed[d, s, 0], mixed[d, s, 1]
                t_real, t_imag = trans[d, s, 0], trans[d, s, 1]
                grads[d, s, 0] = u_real * m_imag - u_imag * m_real
                grads[d, s, 1] = -(u_real * m_real + u_imag * m_imag)
                result.append((t_real * m_real + t_imag * m_imag, t_real * m_imag - t_imag * m_real))
            return tuple(result)

        lax.fori_loop(0, total, backward, backs)

    deeper = valid(1) if depth > 1 else jnp.bool_(False)

    @pl.when(valid(0) & jnp.logical_not(deeper))
    def _():
        run([0])

    if depth > 1:
        @pl.when(deeper)
        def _():
            run(list(range(depth)))


def passed_along(array, axis, by):
    devices = lax.axis_size(axis)
    pairs = [(i, i + by) for i in range(devices) if 0 <= i + by < devices]
    return lax.ppermute(array, axis, pairs)


def params(**more):
    return pltpu.CompilerParams(vmem_limit_bytes=vmem_limit, **more)


def local(phase_map, absorption, probe_wave, measured, rows_at, cols_at, live_mask):
    layers, rows, cols = phase_map.shape
    side = probe_wave.shape[2]
    windows = measured.shape[0]
    slabs = lax.axis_size("slab")
    kept, moved, depth = slot_plan(windows, slabs)
    smem = pl.BlockSpec(memory_space=pltpu.SMEM)
    vmem = pl.BlockSpec(memory_space=pltpu.VMEM)
    f32 = jnp.float32
    dma = pltpu.SemaphoreType.DMA
    pieces = jax.ShapeDtypeStruct((windows, layers, 2, side, side), f32)
    stacked = jax.ShapeDtypeStruct((depth, slabs * layers, 2, side, side), f32)

    index_own = jnp.concatenate([rows_at, cols_at, live_mask])
    index_above = passed_along(index_own, "tile", 1)
    measured_above = passed_along(measured[kept:], "tile", 1)
    own, above = pl.pallas_call(
        cut_kernel,
        out_shape=(pieces, pieces),
        in_specs=[smem, smem, vmem, vmem],
        out_specs=(vmem, vmem),
        scratch_shapes=[pltpu.VMEM((layers, 2, 3 * side, cols), f32)],
        compiler_params=params(),
        name="cut",
    )(index_own, index_above, phase_map, absorption)
    patches = pl.pallas_call(
        gather_kernel,
        out_shape=stacked,
        in_specs=[vmem, vmem],
        out_specs=vmem,
        scratch_shapes=[
            pltpu.VMEM((kept,) + pieces.shape[1:], f32),
            pltpu.VMEM((moved,) + pieces.shape[1:], f32),
            pltpu.VMEM(pieces.shape, f32),
            dma((windows, layers)),
            dma((windows, layers)),
            dma((windows + moved, layers)),
            dma((depth, slabs, layers)),
        ],
        compiler_params=params(collective_id=0, has_side_effects=True),
        name="gather",
    )(own, above)

    mats = [jnp.asarray(m) for m in tables(side)]
    grads = pl.pallas_call(
        wave_kernel,
        out_shape=stacked,
        in_specs=[smem, smem] + [vmem] * (4 + len(mats)),
        out_specs=vmem,
        scratch_shapes=[pltpu.VMEM(stacked.shape, f32), pltpu.VMEM(stacked.shape, f32)],
        compiler_params=params(),
        name="waves",
    )(index_own, index_above, patches, probe_wave, measured, measured_above, *mats)

    own, above = pl.pallas_call(
        scatter_kernel,
        out_shape=(pieces, pieces),
        in_specs=[vmem],
        out_specs=(vmem, vmem),
        scratch_shapes=[
            dma((windows, layers)),
            dma((depth, slabs, layers)),
            dma((windows, layers)),
            dma((windows, layers)),
        ],
        compiler_params=params(collective_id=1, has_side_effects=True),
        name="scatter",
    )(grads)
    whole = jax.ShapeDtypeStruct(phase_map.shape, f32)
    return pl.pallas_call(
        place_kernel,
        out_shape=(whole, whole),
        in_specs=[smem, smem, vmem, vmem],
        out_specs=(vmem, vmem),
        scratch_shapes=[pltpu.VMEM((layers, 2, 3 * side, cols), f32)],
        compiler_params=params(),
        name="place",
    )(index_own, index_above, own, above)


def solution(mesh):
    return jax.shard_map(
        local,
        mesh=mesh,
        in_specs=(
            P(("groups", "slab"), "tile", None),
            P(("groups", "slab"), "tile", None),
            P(),
            P(("groups", "tile"), None, None),
            P(("groups", "tile")),
            P(("groups", "tile")),
            P(("groups", "tile")),
        ),
        out_specs=(P(("groups", "slab"), "tile", None), P(("groups", "slab"), "tile", None)),
        check_vma=False,
    )
```

```python
import functools
import math

import jax
import jax.numpy as jnp
import ml_dtypes
import numpy as np
from jax import lax
from jax.experimental import pallas as pl
from jax.experimental.pallas import tpu as pltpu
from jax.sharding import PartitionSpec as P

chirp_rate = 0.25
MESH = pl.DeviceIdType.MESH
vmem_limit = 56 * 1024 * 1024


def split_host(mat):
    high = mat.astype(np.float32).astype(ml_dtypes.bfloat16)
    low = (mat - high.astype(np.float64)).astype(np.float32).astype(ml_dtypes.bfloat16)
    return high, low


def tables(length):
    index = np.arange(length)
    signed = np.where(index < length // 2, index, index - length).astype(np.float64)
    chirped = -np.pi * chirp_rate * signed * signed / length
    rotation = 2.0 * np.pi * (index[:, None] * index[None, :] % length) / length
    kernel = np.exp(1j * (chirped[:, None] + rotation)).sum(axis=0) / length
    spread = kernel[(index[:, None] - index[None, :]) % length]
    fourier = np.exp(-1j * rotation) / math.sqrt(length)
    forms = []
    for mat in (spread, fourier):
        re, im = mat.real, mat.imag
        minus = np.block([[re, im], [-im, re]])
        plus = np.block([[re, -im], [im, re]])
        for block in (minus, plus):
            high, low = split_host(block)
            forms.append(
                (np.concatenate([high, high, low], axis=0), np.concatenate([high, high, low], axis=1))
            )
    (q_minus, q_plus, f_minus, f_plus) = forms
    return (
        q_plus[1], q_minus[0], q_minus[1], q_plus[0],
        f_plus[1], f_minus[0], f_minus[1], f_plus[0],
    )


def halves(array):
    high = array.astype(jnp.bfloat16)
    low = (array - high.astype(jnp.float32)).astype(jnp.bfloat16)
    return high, low


def sandwich(left_ref, right_ref, waves):
    side = waves[0][0].shape[0]
    high, low = halves(
        jnp.concatenate([jnp.concatenate([re, im], axis=1) for re, im in waves], axis=0)
    )
    beside = jnp.dot(
        jnp.concatenate([high, low, high], axis=1), right_ref[...],
        preferred_element_type=jnp.float32,
    )
    columns = []
    for i in range(len(waves)):
        own = beside[i * side : (i + 1) * side]
        columns.append(jnp.concatenate([own[:, :side], own[:, side:]], axis=0))
    high, low = halves(jnp.concatenate(columns, axis=1) if len(columns) > 1 else columns[0])
    stacked = jnp.dot(
        left_ref[...], jnp.concatenate([high, low, high], axis=0),
        preferred_element_type=jnp.float32,
    )
    return [
        (stacked[:side, i * side : (i + 1) * side], stacked[side:, i * side : (i + 1) * side])
        for i in range(len(waves))
    ]


def cos_sin(angle):
    turns = jnp.floor(angle * (2.0 / math.pi) + 0.5)
    rest = angle - turns * 1.5703125
    rest = rest - turns * 4.837512969970703e-4
    rest = rest - turns * 7.549789948768648e-8
    sq = rest * rest
    sin_part = rest + rest * sq * (-1.6666654611e-1 + sq * (8.3321608736e-3 + sq * -1.9515295891e-4))
    cos_part = 1.0 - 0.5 * sq + sq * sq * (
        4.166664568298827e-2 + sq * (-1.388731625493765e-3 + sq * 2.443315711809948e-5)
    )
    half = jnp.floor(turns * 0.5)
    odd = (turns - 2.0 * half) > 0.5
    flip = 1.0 - 2.0 * (half - 2.0 * jnp.floor(half * 0.5))
    cos_out = jnp.where(odd, -sin_part, cos_part) * flip
    sin_out = jnp.where(odd, cos_part, sin_part) * flip
    return cos_out, sin_out


def column_base(col, side, cols):
    return pl.multiple_of(jnp.minimum(col // side, cols // side - 2) * side, side)


def cut_kernel(above, index_ref, phase_ref, absorb_ref, out_ref, tall):
    windows, layers, _, side, _ = out_ref.shape
    cols = phase_ref.shape[2]
    for layer in range(layers):
        for which, source in enumerate((phase_ref, absorb_ref)):
            parts = [source[layer], jnp.zeros((side, cols), jnp.float32)]
            tall[layer, which, :side] = parts[above]
            tall[layer, which, side:] = parts[1 - above]

    def one(w, carried):
        row, col = index_ref[w], index_ref[windows + w]
        base = column_base(col, side, cols)
        shift = lax.rem(2 * side - (col - base), 2 * side)
        top = pl.multiple_of(row // 8 * 8, 8)
        lift = lax.rem(side + 8 - (row - top), side + 8)
        for layer in range(layers):
            for which in range(2):
                wide = tall[layer, which, pl.ds(top, side + 8), pl.ds(base, 2 * side)]
                narrow = pltpu.roll(wide, shift, 1)[:, :side]
                out_ref[w, layer, which] = pltpu.roll(narrow, lift, 0)[:side]
        return carried

    lax.fori_loop(0, windows, one, 0)


def place_kernel(own_ref, above_ref, own_pieces, above_pieces, out_phase, out_absorb, tall):
    windows, layers, _, side, _ = own_pieces.shape
    cols = out_phase.shape[2]
    tall[...] = jnp.zeros_like(tall)

    def place(index_ref, pieces_ref, start, w):
        row, col = index_ref[w], index_ref[windows + w]
        base = column_base(col, side, cols)
        shift = col - base
        top = pl.multiple_of(row // 8 * 8, 8)
        for layer in range(layers):
            for which in range(2):
                piece = pieces_ref[w, layer, which]
                long = pltpu.roll(jnp.concatenate([piece, jnp.zeros_like(piece[:8])], axis=0), row - top, 0)
                wide = pltpu.roll(jnp.concatenate([long, jnp.zeros_like(long)], axis=1), shift, 1)
                where = (layer, which, pl.ds(start + top, side + 8), pl.ds(base, 2 * side))
                tall[where] = tall[where] + wide

    @pl.loop(0, windows)
    def _(w):
        place(own_ref, own_pieces, side, w)

        @pl.when(lax.axis_index("tile") > 0)
        def _():
            place(above_ref, above_pieces, 0, w)

    for layer in range(layers):
        out_phase[layer] = tall[layer, 0, side : 2 * side]
        out_absorb[layer] = tall[layer, 1, side : 2 * side]


def greet():
    slab, slabs = lax.axis_index("slab"), lax.axis_size("slab")
    tile, tiles = lax.axis_index("tile"), lax.axis_size("tile")
    barrier = pltpu.get_barrier_semaphore()
    for step in range(1, slabs):
        pl.semaphore_signal(
            barrier, inc=1, device_id={"slab": lax.rem(slab + step, slabs)}, device_id_type=MESH
        )

    @pl.when(tile > 0)
    def _():
        pl.semaphore_signal(barrier, inc=1, device_id={"tile": tile - 1}, device_id_type=MESH)

    @pl.when(tile < tiles - 1)
    def _():
        pl.semaphore_signal(barrier, inc=1, device_id={"tile": tile + 1}, device_id_type=MESH)

    beside = (tile > 0).astype(jnp.int32) + (tile < tiles - 1).astype(jnp.int32)
    pl.semaphore_wait(barrier, slabs - 1 + beside)


def slot_plan(windows, slabs):
    moved = windows // 2
    kept = windows - moved
    homes = [(k % slabs, k // slabs) for k in range(windows + moved)]
    if windows % slabs == 0 and 0 < moved <= slabs:
        homes[windows:] = [(j * (slabs // moved), windows // slabs) for j in range(moved)]
    return kept, moved, homes, 1 + max(home[1] for home in homes)


def gather_kernel(
    own, above, measured, patches, measured_above,
    from_below, from_above, merged, zs_sem, zr_sem, xs_sem, xr_sem, ms_sem, mr_sem,
):
    windows, layers = own.shape[:2]
    slab, slabs = lax.axis_index("slab"), lax.axis_size("slab")
    tile, tiles = lax.axis_index("tile"), lax.axis_size("tile")
    kept, moved, homes, _ = slot_plan(windows, slabs)
    first, last = tile == 0, tile == tiles - 1
    greet()

    def up(i, l):
        return pltpu.make_async_remote_copy(
            src_ref=above.at[i, l], dst_ref=from_below.at[i, l], send_sem=zs_sem.at[i, l],
            recv_sem=zr_sem.at[i, l], device_id={"tile": tile - 1}, device_id_type=MESH)

    def down(j, l):
        return pltpu.make_async_remote_copy(
            src_ref=own.at[kept + j, l], dst_ref=from_above.at[j, l], send_sem=zs_sem.at[kept + j, l],
            recv_sem=zr_sem.at[kept + j, l], device_id={"tile": tile + 1}, device_id_type=MESH)

    def data_down(j):
        return pltpu.make_async_remote_copy(
            src_ref=measured.at[kept + j], dst_ref=measured_above.at[j], send_sem=ms_sem.at[j],
            recv_sem=mr_sem.at[j], device_id={"tile": tile + 1}, device_id_type=MESH)

    def across(k, source, l, sender):
        return pltpu.make_async_remote_copy(
            src_ref=source, dst_ref=patches.at[homes[k][1], sender * layers + l], send_sem=xs_sem.at[k, l],
            recv_sem=xr_sem.at[homes[k][1], sender, l], device_id={"slab": homes[k][0]}, device_id_type=MESH)

    @pl.loop(0, layers)
    def _(l):
        @pl.when(jnp.logical_not(first))
        def _():
            for i in range(kept):
                up(i, l).start()

        @pl.when(jnp.logical_not(last))
        def _():
            for j in range(moved):
                down(j, l).start()

    for j in range(moved):
        @pl.when(jnp.logical_not(last) & (slab == homes[kept + j][0]))
        def _():
            data_down(j).start()

    def hand_over(k, source, l):
        @pl.when(slab != homes[k][0])
        def _():
            across(k, source, l, slab).start()

        @pl.when(slab == homes[k][0])
        def _():
            patches[homes[k][1], slab * layers + l] = source[...]

    @pl.when(last)
    def _():
        @pl.loop(0, layers)
        def _(l):
            for j in range(moved):
                hand_over(windows + j, own.at[kept + j, l], l)

    @pl.loop(0, layers)
    def _(l):
        for i in range(kept):
            @pl.when(last)
            def _():
                merged[i, l] = own[i, l]

            @pl.when(jnp.logical_not(last))
            def _():
                up(i, l).wait_recv()
                merged[i, l] = own[i, l] + from_below[i, l]

            hand_over(i, merged.at[i, l], l)

        @pl.when(jnp.logical_not(first))
        def _():
            for j in range(moved):
                down(j, l).wait_recv()
                merged[kept + j, l] = above[kept + j, l] + from_above[j, l]
                hand_over(kept + j, merged.at[kept + j, l], l)

    for j in range(moved):
        @pl.when(jnp.logical_not(last) & (slab == homes[kept + j][0]))
        def _():
            data_down(j).wait_send()

        @pl.when(jnp.logical_not(first) & (slab == homes[kept + j][0]))
        def _():
            data_down(j).wait_recv()

    def finish(k, source):
        @pl.when(slab != homes[k][0])
        def _():
            @pl.loop(0, layers)
            def _(l):
                across(k, source.at[l], l, slab).wait_send()

        @pl.when(slab == homes[k][0])
        def _():
            for sender in range(slabs):
                @pl.when(sender != slab)
                def _():
                    @pl.loop(0, layers)
                    def _(l):
                        across(k, source.at[l], l, sender).wait_recv()

    for i in range(kept):
        finish(i, merged.at[i])

    @pl.when(jnp.logical_not(first))
    def _():
        for j in range(moved):
            finish(kept + j, merged.at[kept + j])

        @pl.loop(0, layers)
        def _(l):
            for i in range(kept):
                up(i, l).wait_send()

    @pl.when(last)
    def _():
        for j in range(moved):
            finish(windows + j, own.at[kept + j])

    @pl.when(jnp.logical_not(last))
    def _():
        @pl.loop(0, layers)
        def _(l):
            for j in range(moved):
                down(j, l).wait_send()


def scatter_kernel(grads, own, above, zs_sem, xs_sem, own_sem, above_sem):
    windows, layers = own.shape[:2]
    slab, slabs = lax.axis_index("slab"), lax.axis_size("slab")
    tile, tiles = lax.axis_index("tile"), lax.axis_size("tile")
    kept, moved, homes, _ = slot_plan(windows, slabs)
    first, last = tile == 0, tile == tiles - 1
    greet()

    def home(k, l):
        if k < kept:
            return own.at[k, l], own_sem.at[k, l]
        if k < windows:
            return above.at[k, l], above_sem.at[k, l]
        return own.at[k - moved, l], own_sem.at[k - moved, l]

    def across(k, l, target):
        place, sem = home(k, l)
        return pltpu.make_async_remote_copy(
            src_ref=grads.at[homes[k][1], target * layers + l], dst_ref=place,
            send_sem=xs_sem.at[homes[k][1], target, l], recv_sem=sem,
            device_id={"slab": target}, device_id_type=MESH)

    def down(i, l):
        return pltpu.make_async_remote_copy(
            src_ref=own.at[i, l], dst_ref=above.at[i, l], send_sem=zs_sem.at[i, l],
            recv_sem=above_sem.at[i, l], device_id={"tile": tile + 1}, device_id_type=MESH)

    def up(k, l):
        return pltpu.make_async_remote_copy(
            src_ref=above.at[k, l], dst_ref=own.at[k, l], send_sem=zs_sem.at[k, l],
            recv_sem=own_sem.at[k, l], device_id={"tile": tile - 1}, device_id_type=MESH)

    def give(k, l):
        @pl.when(slab == homes[k][0])
        def _():
            for target in range(slabs):
                @pl.when(slab != target)
                def _():
                    across(k, l, target).start()

            home(k, l)[0][...] = grads[homes[k][1], slab * layers + l]

    @pl.loop(0, layers)
    def _(l):
        for k in range(kept):
            give(k, l)

        @pl.when(jnp.logical_not(first))
        def _():
            for k in range(kept, windows):
                give(k, l)

        @pl.when(last)
        def _():
            for k in range(windows, windows + moved):
                give(k, l)

    def arrive(k, l):
        @pl.when(slab != homes[k][0])
        def _():
            across(k, l, slab).wait_recv()

    @pl.loop(0, layers)
    def _(l):
        for k in range(kept):
            arrive(k, l)

            @pl.when(jnp.logical_not(last))
            def _():
                down(k, l).start()

        @pl.when(jnp.logical_not(first))
        def _():
            for k in range(kept, windows):
                arrive(k, l)
                up(k, l).start()

    def sent(k, l):
        @pl.when(slab == homes[k][0])
        def _():
            for target in range(slabs):
                @pl.when(slab != target)
                def _():
                    across(k, l, target).wait_send()

    @pl.loop(0, layers)
    def _(l):
        for k in range(kept):
            sent(k, l)

        @pl.when(jnp.logical_not(first))
        def _():
            for k in range(kept, windows):
                sent(k, l)
                up(k, l).wait_send()
            for k in range(kept):
                down(k, l).wait_recv()

        @pl.when(jnp.logical_not(last))
        def _():
            for k in range(kept):
                down(k, l).wait_send()
            for k in range(kept, windows):
                up(k, l).wait_recv()

        @pl.when(last)
        def _():
            for k in range(windows, windows + moved):
                arrive(k, l)
                sent(k, l)


def wave_kernel(
    own_ref, above_ref, patches, probe_ref, measured_ref, above_measured_ref,
    q_left, q_right, qa_left, qa_right, f_left, f_right, fa_left, fa_right,
    grads, trans, mixed,
):
    depth, total, _, side, _ = patches.shape
    windows = measured_ref.shape[0]
    slab, slabs = lax.axis_index("slab"), lax.axis_size("slab")
    tile, tiles = lax.axis_index("tile"), lax.axis_size("tile")
    kept, moved, homes, _ = slot_plan(windows, slabs)

    def slot_at(d):
        slot = jnp.int32(-1)
        for k, (home_slab, home_depth) in enumerate(homes):
            if home_depth == d:
                slot = jnp.where(slab == home_slab, k, slot)
        return slot

    def valid(d):
        k = slot_at(d)
        mine = (k >= 0) & (k < kept)
        from_above = (k >= kept) & (k < windows) & (tile > 0)
        extra = (k >= windows) & (tile == tiles - 1)
        return mine | from_above | extra

    def excess_wave(d, wave):
        k = slot_at(d)
        is_above = (k >= kept) & (k < windows)
        own_at = jnp.clip(jnp.where(k < windows, k, k - moved), 0, windows - 1)
        above_at = jnp.clip(k, kept, windows - 1)
        live = jnp.where(is_above, above_ref[2 * windows + above_at], own_ref[2 * windows + own_at])
        target = jnp.where(is_above, above_measured_ref[above_at - kept], measured_ref[own_at])
        far_real, far_imag = wave
        excess = (0.5 * live.astype(jnp.float32)) * (far_real * far_real + far_imag * far_imag - target)
        return excess * far_real, excess * far_imag

    def run(slots):
        def prepare(s):
            for d in slots:
                damping = jnp.exp(-patches[d, s, 1])
                cos_part, sin_part = cos_sin(patches[d, s, 0])
                trans[d, s, 0] = damping * cos_part
                trans[d, s, 1] = damping * sin_part

        prepare(0)

        def forward(s, waves):
            entering = []
            for d, (wave_real, wave_imag) in zip(slots, waves):
                t_real, t_imag = trans[d, s, 0], trans[d, s, 1]
                mixed_real = t_real * wave_real - t_imag * wave_imag
                mixed_imag = t_real * wave_imag + t_imag * wave_real
                mixed[d, s, 0] = mixed_real
                mixed[d, s, 1] = mixed_imag
                entering.append((mixed_real, mixed_imag))
            leaving = sandwich(q_left, q_right, entering)
            prepare(jnp.minimum(s + 1, total - 1))
            return tuple(leaving)

        waves = lax.fori_loop(0, total, forward, tuple((probe_ref[0], probe_ref[1]) for d in slots))
        far = sandwich(f_left, f_right, waves)
        seeds = [excess_wave(d, wave) for d, wave in zip(slots, far)]
        backs = tuple(sandwich(fa_left, fa_right, seeds))

        def backward(i, backs):
            s = total - 1 - i
            result = []
            for d, (m_real, m_imag) in zip(slots, sandwich(qa_left, qa_right, backs)):
                u_real, u_imag = mixed[d, s, 0], mixed[d, s, 1]
                t_real, t_imag = trans[d, s, 0], trans[d, s, 1]
                grads[d, s, 0] = u_real * m_imag - u_imag * m_real
                grads[d, s, 1] = -(u_real * m_real + u_imag * m_imag)
                result.append((t_real * m_real + t_imag * m_imag, t_real * m_imag - t_imag * m_real))
            return tuple(result)

        lax.fori_loop(0, total, backward, backs)

    deeper = valid(1) if depth > 1 else jnp.bool_(False)

    @pl.when(valid(0) & jnp.logical_not(deeper))
    def _():
        run([0])

    if depth > 1:
        @pl.when(deeper)
        def _():
            run(list(range(depth)))


def passed_along(array, axis, by):
    devices = lax.axis_size(axis)
    pairs = [(i, i + by) for i in range(devices) if 0 <= i + by < devices]
    return lax.ppermute(array, axis, pairs)


def params(**more):
    return pltpu.CompilerParams(vmem_limit_bytes=vmem_limit, **more)


def local(phase_map, absorption, probe_wave, measured, rows_at, cols_at, live_mask):
    layers, rows, cols = phase_map.shape
    side = probe_wave.shape[2]
    windows = measured.shape[0]
    slabs = lax.axis_size("slab")
    kept, moved, homes, depth = slot_plan(windows, slabs)
    smem = pl.BlockSpec(memory_space=pltpu.SMEM)
    vmem = pl.BlockSpec(memory_space=pltpu.VMEM)
    f32 = jnp.float32
    dma = pltpu.SemaphoreType.DMA
    pieces = jax.ShapeDtypeStruct((windows, layers, 2, side, side), f32)
    stacked = jax.ShapeDtypeStruct((depth, slabs * layers, 2, side, side), f32)

    index_own = jnp.concatenate([rows_at, cols_at, live_mask])
    index_above = passed_along(index_own, "tile", 1)
    own, above = (
        pl.pallas_call(
            functools.partial(cut_kernel, which),
            out_shape=pieces,
            in_specs=[smem, vmem, vmem],
            out_specs=vmem,
            scratch_shapes=[pltpu.VMEM((layers, 2, 2 * side, cols), f32)],
            compiler_params=params(),
            cost_estimate=pl.CostEstimate(
                flops=0, bytes_accessed=8 * layers * side * (cols + windows * side), transcendentals=0
            ),
            name=name,
        )(index, phase_map, absorption)
        for which, name, index in ((0, "cut_own", index_own), (1, "cut_above", index_above))
    )
    patches, measured_above = pl.pallas_call(
        gather_kernel,
        out_shape=(stacked, jax.ShapeDtypeStruct((moved, side, side), f32)),
        in_specs=[vmem, vmem, vmem],
        out_specs=(vmem, vmem),
        scratch_shapes=[
            pltpu.VMEM((kept,) + pieces.shape[1:], f32),
            pltpu.VMEM((moved,) + pieces.shape[1:], f32),
            pltpu.VMEM(pieces.shape, f32),
            dma((windows, layers)),
            dma((windows, layers)),
            dma((windows + moved, layers)),
            dma((depth, slabs, layers)),
            dma((moved,)),
            dma((moved,)),
        ],
        compiler_params=params(collective_id=0, has_side_effects=True),
        name="gather",
    )(own, above, measured)

    mats = [jnp.asarray(m) for m in tables(side)]
    grads = pl.pallas_call(
        wave_kernel,
        out_shape=stacked,
        in_specs=[smem, smem] + [vmem] * (4 + len(mats)),
        out_specs=vmem,
        scratch_shapes=[pltpu.VMEM(stacked.shape, f32), pltpu.VMEM(stacked.shape, f32)],
        compiler_params=params(),
        name="waves",
    )(index_own, index_above, patches, probe_wave, measured, measured_above, *mats)

    own, above = pl.pallas_call(
        scatter_kernel,
        out_shape=(pieces, pieces),
        in_specs=[vmem],
        out_specs=(vmem, vmem),
        scratch_shapes=[
            dma((windows, layers)),
            dma((depth, slabs, layers)),
            dma((windows, layers)),
            dma((windows, layers)),
        ],
        compiler_params=params(collective_id=1, has_side_effects=True),
        name="scatter",
    )(grads)
    whole = jax.ShapeDtypeStruct(phase_map.shape, f32)
    return pl.pallas_call(
        place_kernel,
        out_shape=(whole, whole),
        in_specs=[smem, smem, vmem, vmem],
        out_specs=(vmem, vmem),
        scratch_shapes=[pltpu.VMEM((layers, 2, 3 * side, cols), f32)],
        compiler_params=params(),
        name="place",
    )(index_own, index_above, own, above)


def solution(mesh):
    return jax.shard_map(
        local,
        mesh=mesh,
        in_specs=(
            P(("groups", "slab"), "tile", None),
            P(("groups", "slab"), "tile", None),
            P(),
            P(("groups", "tile"), None, None),
            P(("groups", "tile")),
            P(("groups", "tile")),
            P(("groups", "tile")),
        ),
        out_specs=(P(("groups", "slab"), "tile", None), P(("groups", "slab"), "tile", None)),
        check_vma=False,
    )
```

```python
import functools
import math

import jax
import jax.numpy as jnp
import ml_dtypes
import numpy as np
from jax import lax
from jax.experimental import pallas as pl
from jax.experimental.pallas import tpu as pltpu
from jax.sharding import PartitionSpec as P

chirp_rate = 0.25
MESH = pl.DeviceIdType.MESH
vmem_limit = 56 * 1024 * 1024


def split_host(mat):
    high = mat.astype(np.float32).astype(ml_dtypes.bfloat16)
    low = (mat - high.astype(np.float64)).astype(np.float32).astype(ml_dtypes.bfloat16)
    return high, low


def tables(length):
    index = np.arange(length)
    signed = np.where(index < length // 2, index, index - length).astype(np.float64)
    chirped = -np.pi * chirp_rate * signed * signed / length
    rotation = 2.0 * np.pi * (index[:, None] * index[None, :] % length) / length
    kernel = np.exp(1j * (chirped[:, None] + rotation)).sum(axis=0) / length
    spread = kernel[(index[:, None] - index[None, :]) % length]
    fourier = np.exp(-1j * rotation) / math.sqrt(length)
    forms = []
    for mat in (spread, fourier):
        re, im = mat.real, mat.imag
        minus = np.block([[re, im], [-im, re]])
        plus = np.block([[re, -im], [im, re]])
        for block in (minus, plus):
            high, low = split_host(block)
            forms.append(
                (np.concatenate([high, high, low], axis=0), np.concatenate([high, high, low], axis=1))
            )
    (q_minus, q_plus, f_minus, f_plus) = forms
    return (
        q_plus[1], q_minus[0], q_minus[1], q_plus[0],
        f_plus[1], f_minus[0], f_minus[1], f_plus[0],
    )


def halves(array):
    high = array.astype(jnp.bfloat16)
    low = (array - high.astype(jnp.float32)).astype(jnp.bfloat16)
    return high, low


def sandwich(left_ref, right_ref, waves):
    side = waves[0][0].shape[0]
    high, low = halves(
        jnp.concatenate([jnp.concatenate([re, im], axis=1) for re, im in waves], axis=0)
    )
    beside = jnp.dot(
        jnp.concatenate([high, low, high], axis=1), right_ref[...],
        preferred_element_type=jnp.float32,
    )
    columns = []
    for i in range(len(waves)):
        own = beside[i * side : (i + 1) * side]
        columns.append(jnp.concatenate([own[:, :side], own[:, side:]], axis=0))
    high, low = halves(jnp.concatenate(columns, axis=1) if len(columns) > 1 else columns[0])
    stacked = jnp.dot(
        left_ref[...], jnp.concatenate([high, low, high], axis=0),
        preferred_element_type=jnp.float32,
    )
    return [
        (stacked[:side, i * side : (i + 1) * side], stacked[side:, i * side : (i + 1) * side])
        for i in range(len(waves))
    ]


def cos_sin(angle):
    turns = jnp.floor(angle * (2.0 / math.pi) + 0.5)
    rest = angle - turns * 1.5703125
    rest = rest - turns * 4.837512969970703e-4
    rest = rest - turns * 7.549789948768648e-8
    sq = rest * rest
    sin_part = rest + rest * sq * (-1.6666654611e-1 + sq * (8.3321608736e-3 + sq * -1.9515295891e-4))
    cos_part = 1.0 - 0.5 * sq + sq * sq * (
        4.166664568298827e-2 + sq * (-1.388731625493765e-3 + sq * 2.443315711809948e-5)
    )
    half = jnp.floor(turns * 0.5)
    odd = (turns - 2.0 * half) > 0.5
    flip = 1.0 - 2.0 * (half - 2.0 * jnp.floor(half * 0.5))
    cos_out = jnp.where(odd, -sin_part, cos_part) * flip
    sin_out = jnp.where(odd, cos_part, sin_part) * flip
    return cos_out, sin_out


def column_base(col, side, cols):
    return pl.multiple_of(jnp.minimum(col // side, cols // side - 2) * side, side)


def cut_kernel(above, index_ref, phase_ref, absorb_ref, out_ref, tall):
    windows, layers, _, side, _ = out_ref.shape
    cols = phase_ref.shape[2]
    for layer in range(layers):
        for which, source in enumerate((phase_ref, absorb_ref)):
            parts = [source[layer], jnp.zeros((side, cols), jnp.float32)]
            tall[layer, which, :side] = parts[above]
            tall[layer, which, side:] = parts[1 - above]

    def one(w, carried):
        row, col = index_ref[w], index_ref[windows + w]
        base = column_base(col, side, cols)
        shift = lax.rem(2 * side - (col - base), 2 * side)
        top = pl.multiple_of(row // 8 * 8, 8)
        lift = lax.rem(side + 8 - (row - top), side + 8)
        for layer in range(layers):
            for which in range(2):
                wide = tall[layer, which, pl.ds(top, side + 8), pl.ds(base, 2 * side)]
                narrow = pltpu.roll(wide, shift, 1)[:, :side]
                out_ref[w, layer, which] = pltpu.roll(narrow, lift, 0)[:side]
        return carried

    lax.fori_loop(0, windows, one, 0)


def place_kernel(own_ref, above_ref, own_pieces, above_pieces, out_phase, out_absorb, tall):
    windows, layers, _, side, _ = own_pieces.shape
    cols = out_phase.shape[2]
    tall[...] = jnp.zeros_like(tall)

    def place(index_ref, pieces_ref, start, w):
        row, col = index_ref[w], index_ref[windows + w]
        base = column_base(col, side, cols)
        shift = col - base
        top = pl.multiple_of(row // 8 * 8, 8)
        for layer in range(layers):
            for which in range(2):
                piece = pieces_ref[w, layer, which]
                long = pltpu.roll(jnp.concatenate([piece, jnp.zeros_like(piece[:8])], axis=0), row - top, 0)
                wide = pltpu.roll(jnp.concatenate([long, jnp.zeros_like(long)], axis=1), shift, 1)
                where = (layer, which, pl.ds(start + top, side + 8), pl.ds(base, 2 * side))
                tall[where] = tall[where] + wide

    @pl.loop(0, windows)
    def _(w):
        place(own_ref, own_pieces, side, w)

        @pl.when(lax.axis_index("tile") > 0)
        def _():
            place(above_ref, above_pieces, 0, w)

    for layer in range(layers):
        out_phase[layer] = tall[layer, 0, side : 2 * side]
        out_absorb[layer] = tall[layer, 1, side : 2 * side]


def greet():
    slab, slabs = lax.axis_index("slab"), lax.axis_size("slab")
    tile, tiles = lax.axis_index("tile"), lax.axis_size("tile")
    barrier = pltpu.get_barrier_semaphore()
    for step in range(1, slabs):
        pl.semaphore_signal(
            barrier, inc=1, device_id={"slab": lax.rem(slab + step, slabs)}, device_id_type=MESH
        )

    @pl.when(tile > 0)
    def _():
        pl.semaphore_signal(barrier, inc=1, device_id={"tile": tile - 1}, device_id_type=MESH)

    @pl.when(tile < tiles - 1)
    def _():
        pl.semaphore_signal(barrier, inc=1, device_id={"tile": tile + 1}, device_id_type=MESH)

    beside = (tile > 0).astype(jnp.int32) + (tile < tiles - 1).astype(jnp.int32)
    pl.semaphore_wait(barrier, slabs - 1 + beside)


def slot_plan(windows, slabs):
    moved = windows // 2
    kept = windows - moved
    lanes = slabs // 2
    homes = [(k % lanes, k // lanes) for k in range(windows + moved)]
    return kept, moved, homes, 1 + max(home[1] for home in homes), lanes


def gather_kernel(
    own, above, measured, patches, measured_above,
    from_below, from_above, merged, zs_sem, zr_sem, xs_sem, xr_sem, ms_sem, mr_sem,
):
    windows, layers = own.shape[:2]
    slab, slabs = lax.axis_index("slab"), lax.axis_size("slab")
    tile, tiles = lax.axis_index("tile"), lax.axis_size("tile")
    kept, moved, homes, _, lanes = slot_plan(windows, slabs)
    half, lane = slab // lanes, lax.rem(slab, lanes)
    first, last = tile == 0, tile == tiles - 1
    greet()

    def up(i, l):
        return pltpu.make_async_remote_copy(
            src_ref=above.at[i, l], dst_ref=from_below.at[i, l], send_sem=zs_sem.at[i, l],
            recv_sem=zr_sem.at[i, l], device_id={"tile": tile - 1}, device_id_type=MESH)

    def down(j, l):
        return pltpu.make_async_remote_copy(
            src_ref=own.at[kept + j, l], dst_ref=from_above.at[j, l], send_sem=zs_sem.at[kept + j, l],
            recv_sem=zr_sem.at[kept + j, l], device_id={"tile": tile + 1}, device_id_type=MESH)

    def data_down(j):
        return pltpu.make_async_remote_copy(
            src_ref=measured.at[kept + j], dst_ref=measured_above.at[j], send_sem=ms_sem.at[j],
            recv_sem=mr_sem.at[j], device_id={"tile": tile + 1}, device_id_type=MESH)

    def across(k, source, l, sender):
        return pltpu.make_async_remote_copy(
            src_ref=source, dst_ref=patches.at[homes[k][1], sender * layers + l], send_sem=xs_sem.at[k, l],
            recv_sem=xr_sem.at[homes[k][1], sender, l], device_id={"slab": half * lanes + homes[k][0]}, device_id_type=MESH)

    @pl.loop(0, layers)
    def _(l):
        @pl.when(jnp.logical_not(first))
        def _():
            for i in range(kept):
                up(i, l).start()

        @pl.when(jnp.logical_not(last))
        def _():
            for j in range(moved):
                down(j, l).start()

    for j in range(moved):
        @pl.when(jnp.logical_not(last) & (lane == homes[kept + j][0]))
        def _():
            data_down(j).start()

    def hand_over(k, source, l):
        @pl.when(lane != homes[k][0])
        def _():
            across(k, source, l, lane).start()

        @pl.when(lane == homes[k][0])
        def _():
            patches[homes[k][1], lane * layers + l] = source[...]

    @pl.when(last)
    def _():
        @pl.loop(0, layers)
        def _(l):
            for j in range(moved):
                hand_over(windows + j, own.at[kept + j, l], l)

    @pl.loop(0, layers)
    def _(l):
        for i in range(kept):
            @pl.when(last)
            def _():
                merged[i, l] = own[i, l]

            @pl.when(jnp.logical_not(last))
            def _():
                up(i, l).wait_recv()
                merged[i, l] = own[i, l] + from_below[i, l]

            hand_over(i, merged.at[i, l], l)

        @pl.when(jnp.logical_not(first))
        def _():
            for j in range(moved):
                down(j, l).wait_recv()
                merged[kept + j, l] = above[kept + j, l] + from_above[j, l]
                hand_over(kept + j, merged.at[kept + j, l], l)

    for j in range(moved):
        @pl.when(jnp.logical_not(last) & (lane == homes[kept + j][0]))
        def _():
            data_down(j).wait_send()

        @pl.when(jnp.logical_not(first) & (lane == homes[kept + j][0]))
        def _():
            data_down(j).wait_recv()

    def finish(k, source):
        @pl.when(lane != homes[k][0])
        def _():
            @pl.loop(0, layers)
            def _(l):
                across(k, source.at[l], l, lane).wait_send()

        @pl.when(lane == homes[k][0])
        def _():
            for sender in range(lanes):
                @pl.when(sender != lane)
                def _():
                    @pl.loop(0, layers)
                    def _(l):
                        across(k, source.at[l], l, sender).wait_recv()

    for i in range(kept):
        finish(i, merged.at[i])

    @pl.when(jnp.logical_not(first))
    def _():
        for j in range(moved):
            finish(kept + j, merged.at[kept + j])

        @pl.loop(0, layers)
        def _(l):
            for i in range(kept):
                up(i, l).wait_send()

    @pl.when(last)
    def _():
        for j in range(moved):
            finish(windows + j, own.at[kept + j])

    @pl.when(jnp.logical_not(last))
    def _():
        @pl.loop(0, layers)
        def _(l):
            for j in range(moved):
                down(j, l).wait_send()


def scatter_kernel(grads, own, above, zs_sem, xs_sem, own_sem, above_sem):
    windows, layers = own.shape[:2]
    slab, slabs = lax.axis_index("slab"), lax.axis_size("slab")
    tile, tiles = lax.axis_index("tile"), lax.axis_size("tile")
    kept, moved, homes, _, lanes = slot_plan(windows, slabs)
    half, lane = slab // lanes, lax.rem(slab, lanes)
    first, last = tile == 0, tile == tiles - 1
    greet()

    def home(k, l):
        if k < kept:
            return own.at[k, l], own_sem.at[k, l]
        if k < windows:
            return above.at[k, l], above_sem.at[k, l]
        return own.at[k - moved, l], own_sem.at[k - moved, l]

    def across(k, l, target):
        place, sem = home(k, l)
        return pltpu.make_async_remote_copy(
            src_ref=grads.at[homes[k][1], target * layers + l], dst_ref=place,
            send_sem=xs_sem.at[homes[k][1], target, l], recv_sem=sem,
            device_id={"slab": half * lanes + target}, device_id_type=MESH)

    def down(i, l):
        return pltpu.make_async_remote_copy(
            src_ref=own.at[i, l], dst_ref=above.at[i, l], send_sem=zs_sem.at[i, l],
            recv_sem=above_sem.at[i, l], device_id={"tile": tile + 1}, device_id_type=MESH)

    def up(k, l):
        return pltpu.make_async_remote_copy(
            src_ref=above.at[k, l], dst_ref=own.at[k, l], send_sem=zs_sem.at[k, l],
            recv_sem=own_sem.at[k, l], device_id={"tile": tile - 1}, device_id_type=MESH)

    def give(k, l):
        @pl.when(lane == homes[k][0])
        def _():
            for target in range(lanes):
                @pl.when(lane != target)
                def _():
                    across(k, l, target).start()

            home(k, l)[0][...] = grads[homes[k][1], lane * layers + l]

    @pl.loop(0, layers)
    def _(l):
        for k in range(kept):
            give(k, l)

        @pl.when(jnp.logical_not(first))
        def _():
            for k in range(kept, windows):
                give(k, l)

        @pl.when(last)
        def _():
            for k in range(windows, windows + moved):
                give(k, l)

    def arrive(k, l):
        @pl.when(lane != homes[k][0])
        def _():
            across(k, l, lane).wait_recv()

    @pl.loop(0, layers)
    def _(l):
        for k in range(kept):
            arrive(k, l)

            @pl.when(jnp.logical_not(last))
            def _():
                down(k, l).start()

        @pl.when(jnp.logical_not(first))
        def _():
            for k in range(kept, windows):
                arrive(k, l)
                up(k, l).start()

    def sent(k, l):
        @pl.when(lane == homes[k][0])
        def _():
            for target in range(lanes):
                @pl.when(lane != target)
                def _():
                    across(k, l, target).wait_send()

    @pl.loop(0, layers)
    def _(l):
        for k in range(kept):
            sent(k, l)

        @pl.when(jnp.logical_not(first))
        def _():
            for k in range(kept, windows):
                sent(k, l)
                up(k, l).wait_send()
            for k in range(kept):
                down(k, l).wait_recv()

        @pl.when(jnp.logical_not(last))
        def _():
            for k in range(kept):
                down(k, l).wait_send()
            for k in range(kept, windows):
                up(k, l).wait_recv()

        @pl.when(last)
        def _():
            for k in range(windows, windows + moved):
                arrive(k, l)
                sent(k, l)


def wave_kernel(
    own_ref, above_ref, patches, probe_ref, measured_ref, above_measured_ref,
    q_left, q_right, qa_left, qa_right, f_left, f_right, fa_left, fa_right,
    grads, trans, mixed, leaving, arriving, send_sem, recv_sem,
):
    depth, total, _, side, _ = patches.shape
    windows = measured_ref.shape[0]
    slab, slabs = lax.axis_index("slab"), lax.axis_size("slab")
    tile, tiles = lax.axis_index("tile"), lax.axis_size("tile")
    kept, moved, homes, _, lanes = slot_plan(windows, slabs)
    half, lane = slab // lanes, lax.rem(slab, lanes)

    def slot_at(d):
        slot = jnp.int32(-1)
        for k, (home_slab, home_depth) in enumerate(homes):
            if home_depth == d:
                slot = jnp.where(lane == home_slab, k, slot)
        return slot

    def valid(d):
        k = slot_at(d)
        mine = (k >= 0) & (k < kept)
        from_above = (k >= kept) & (k < windows) & (tile > 0)
        extra = (k >= windows) & (tile == tiles - 1)
        return mine | from_above | extra

    def excess_wave(d, wave):
        k = slot_at(d)
        is_above = (k >= kept) & (k < windows)
        own_at = jnp.clip(jnp.where(k < windows, k, k - moved), 0, windows - 1)
        above_at = jnp.clip(k, kept, windows - 1)
        live = jnp.where(is_above, above_ref[2 * windows + above_at], own_ref[2 * windows + own_at])
        target = jnp.where(is_above, above_measured_ref[above_at - kept], measured_ref[own_at])
        far_real, far_imag = wave
        excess = (0.5 * live.astype(jnp.float32)) * (far_real * far_real + far_imag * far_imag - target)
        return excess * far_real, excess * far_imag

    def run(slots):
        def prepare(s):
            for d in slots:
                damping = jnp.exp(-patches[d, s, 1])
                cos_part, sin_part = cos_sin(patches[d, s, 0])
                trans[d, s, 0] = damping * cos_part
                trans[d, s, 1] = damping * sin_part

        prepare(0)

        def forward(s, waves):
            entering = []
            for d, (wave_real, wave_imag) in zip(slots, waves):
                t_real, t_imag = trans[d, s, 0], trans[d, s, 1]
                mixed_real = t_real * wave_real - t_imag * wave_imag
                mixed_imag = t_real * wave_imag + t_imag * wave_real
                mixed[d, s, 0] = mixed_real
                mixed[d, s, 1] = mixed_imag
                entering.append((mixed_real, mixed_imag))
            leaving = sandwich(q_left, q_right, entering)
            prepare(jnp.minimum(s + 1, total - 1))
            return tuple(leaving)

        def hop(target):
            return [
                pltpu.make_async_remote_copy(
                    src_ref=leaving.at[d], dst_ref=arriving.at[d], send_sem=send_sem.at[d],
                    recv_sem=recv_sem.at[d], device_id={"slab": target}, device_id_type=MESH)
                for d in slots
            ]

        def pass_on(waves, target):
            for d, wave, copy in zip(slots, waves, hop(target)):
                leaving[d, 0] = wave[0]
                leaving[d, 1] = wave[1]
                copy.start()

        def arrived():
            for copy in hop(other):
                copy.wait_recv()
            return tuple((arriving[d, 0], arriving[d, 1]) for d in slots)

        def backward(i, backs):
            s = total - 1 - i
            result = []
            for d, (m_real, m_imag) in zip(slots, sandwich(qa_left, qa_right, backs)):
                u_real, u_imag = mixed[d, s, 0], mixed[d, s, 1]
                t_real, t_imag = trans[d, s, 0], trans[d, s, 1]
                grads[d, s, 0] = u_real * m_imag - u_imag * m_real
                grads[d, s, 1] = -(u_real * m_real + u_imag * m_imag)
                result.append((t_real * m_real + t_imag * m_imag, t_real * m_imag - t_imag * m_real))
            return tuple(result)

        @pl.when(half == 0)
        def _():
            start = tuple((probe_ref[0], probe_ref[1]) for d in slots)
            pass_on(lax.fori_loop(0, total, forward, start), other)
            backs = arrived()
            lax.fori_loop(0, total, backward, backs)

        @pl.when(half == 1)
        def _():
            waves = lax.fori_loop(0, total, forward, arrived())
            far = sandwich(f_left, f_right, waves)
            seeds = [excess_wave(d, wave) for d, wave in zip(slots, far)]
            backs = tuple(sandwich(fa_left, fa_right, seeds))
            pass_on(lax.fori_loop(0, total, backward, backs), other)

        for copy in hop(other):
            copy.wait_send()

    other = jnp.where(half == 0, slab + lanes, slab - lanes)
    barrier = pltpu.get_barrier_semaphore()
    pl.semaphore_signal(barrier, inc=1, device_id={"slab": other}, device_id_type=MESH)
    pl.semaphore_wait(barrier, 1)
    filled = jnp.int32(0)
    for d in range(depth):
        filled = jnp.where(valid(d), d + 1, filled)
    for count in range(1, depth + 1):
        @pl.when(filled == count)
        def _():
            run(list(range(count)))


def passed_along(array, axis, by):
    devices = lax.axis_size(axis)
    pairs = [(i, i + by) for i in range(devices) if 0 <= i + by < devices]
    return lax.ppermute(array, axis, pairs)


def params(**more):
    return pltpu.CompilerParams(vmem_limit_bytes=vmem_limit, **more)


def local(phase_map, absorption, probe_wave, measured, rows_at, cols_at, live_mask):
    layers, rows, cols = phase_map.shape
    side = probe_wave.shape[2]
    windows = measured.shape[0]
    slabs = lax.axis_size("slab")
    kept, moved, homes, depth, lanes = slot_plan(windows, slabs)
    smem = pl.BlockSpec(memory_space=pltpu.SMEM)
    vmem = pl.BlockSpec(memory_space=pltpu.VMEM)
    f32 = jnp.float32
    dma = pltpu.SemaphoreType.DMA
    pieces = jax.ShapeDtypeStruct((windows, layers, 2, side, side), f32)
    stacked = jax.ShapeDtypeStruct((depth, lanes * layers, 2, side, side), f32)

    index_own = jnp.concatenate([rows_at, cols_at, live_mask])
    index_above = passed_along(index_own, "tile", 1)
    own, above = (
        pl.pallas_call(
            functools.partial(cut_kernel, which),
            out_shape=pieces,
            in_specs=[smem, vmem, vmem],
            out_specs=vmem,
            scratch_shapes=[pltpu.VMEM((layers, 2, 2 * side, cols), f32)],
            compiler_params=params(),
            cost_estimate=pl.CostEstimate(
                flops=0, bytes_accessed=8 * layers * side * (cols + windows * side), transcendentals=0
            ),
            name=name,
        )(index, phase_map, absorption)
        for which, name, index in ((0, "cut_own", index_own), (1, "cut_above", index_above))
    )
    patches, measured_above = pl.pallas_call(
        gather_kernel,
        out_shape=(stacked, jax.ShapeDtypeStruct((moved, side, side), f32)),
        in_specs=[vmem, vmem, vmem],
        out_specs=(vmem, vmem),
        scratch_shapes=[
            pltpu.VMEM((kept,) + pieces.shape[1:], f32),
            pltpu.VMEM((moved,) + pieces.shape[1:], f32),
            pltpu.VMEM(pieces.shape, f32),
            dma((windows, layers)),
            dma((windows, layers)),
            dma((windows + moved, layers)),
            dma((depth, lanes, layers)),
            dma((moved,)),
            dma((moved,)),
        ],
        compiler_params=params(collective_id=0, has_side_effects=True),
        name="gather",
    )(own, above, measured)

    mats = [jnp.asarray(m) for m in tables(side)]
    grads = pl.pallas_call(
        wave_kernel,
        out_shape=stacked,
        in_specs=[smem, smem] + [vmem] * (4 + len(mats)),
        out_specs=vmem,
        scratch_shapes=[
            pltpu.VMEM(stacked.shape, f32),
            pltpu.VMEM(stacked.shape, f32),
            pltpu.VMEM((depth, 2, side, side), f32),
            pltpu.VMEM((depth, 2, side, side), f32),
            dma((depth,)),
            dma((depth,)),
        ],
        compiler_params=params(collective_id=2, has_side_effects=True),
        name="waves",
    )(index_own, index_above, patches, probe_wave, measured, measured_above, *mats)

    own, above = pl.pallas_call(
        scatter_kernel,
        out_shape=(pieces, pieces),
        in_specs=[vmem],
        out_specs=(vmem, vmem),
        scratch_shapes=[
            dma((windows, layers)),
            dma((depth, lanes, layers)),
            dma((windows, layers)),
            dma((windows, layers)),
        ],
        compiler_params=params(collective_id=1, has_side_effects=True),
        name="scatter",
    )(grads)
    whole = jax.ShapeDtypeStruct(phase_map.shape, f32)
    return pl.pallas_call(
        place_kernel,
        out_shape=(whole, whole),
        in_specs=[smem, smem, vmem, vmem],
        out_specs=(vmem, vmem),
        scratch_shapes=[pltpu.VMEM((layers, 2, 3 * side, cols), f32)],
        compiler_params=params(),
        name="place",
    )(index_own, index_above, own, above)


def solution(mesh):
    return jax.shard_map(
        local,
        mesh=mesh,
        in_specs=(
            P(("groups", "slab"), "tile", None),
            P(("groups", "slab"), "tile", None),
            P(),
            P(("groups", "tile"), None, None),
            P(("groups", "tile")),
            P(("groups", "tile")),
            P(("groups", "tile")),
        ),
        out_specs=(P(("groups", "slab"), "tile", None), P(("groups", "slab"), "tile", None)),
        check_vma=False,
    )
```

```python
import functools
import math

import jax
import jax.numpy as jnp
import ml_dtypes
import numpy as np
from jax import lax
from jax.experimental import pallas as pl
from jax.experimental.pallas import tpu as pltpu
from jax.sharding import PartitionSpec as P

chirp_rate = 0.25
MESH = pl.DeviceIdType.MESH
vmem_limit = 56 * 1024 * 1024


def split_host(mat):
    high = mat.astype(np.float32).astype(ml_dtypes.bfloat16)
    low = (mat - high.astype(np.float64)).astype(np.float32).astype(ml_dtypes.bfloat16)
    return high, low


def tables(length):
    index = np.arange(length)
    signed = np.where(index < length // 2, index, index - length).astype(np.float64)
    chirped = -np.pi * chirp_rate * signed * signed / length
    rotation = 2.0 * np.pi * (index[:, None] * index[None, :] % length) / length
    kernel = np.exp(1j * (chirped[:, None] + rotation)).sum(axis=0) / length
    spread = kernel[(index[:, None] - index[None, :]) % length]
    fourier = np.exp(-1j * rotation) / math.sqrt(length)
    forms = []
    for mat in (spread, fourier):
        re, im = mat.real, mat.imag
        minus = np.block([[re, im], [-im, re]])
        plus = np.block([[re, -im], [im, re]])
        for block in (minus, plus):
            high, low = split_host(block)
            forms.append(
                (np.concatenate([high, high, low], axis=0), np.concatenate([high, high, low], axis=1))
            )
    (q_minus, q_plus, f_minus, f_plus) = forms
    return (
        q_plus[1], q_minus[0], q_minus[1], q_plus[0],
        f_plus[1], f_minus[0], f_minus[1], f_plus[0],
    )


def halves(array):
    high = array.astype(jnp.bfloat16)
    low = (array - high.astype(jnp.float32)).astype(jnp.bfloat16)
    return high, low


def sandwich(left_ref, right_ref, waves):
    side = waves[0][0].shape[0]
    high, low = halves(
        jnp.concatenate([jnp.concatenate([re, im], axis=1) for re, im in waves], axis=0)
    )
    beside = jnp.dot(
        jnp.concatenate([high, low, high], axis=1), right_ref[...],
        preferred_element_type=jnp.float32,
    )
    columns = []
    for i in range(len(waves)):
        own = beside[i * side : (i + 1) * side]
        columns.append(jnp.concatenate([own[:, :side], own[:, side:]], axis=0))
    high, low = halves(jnp.concatenate(columns, axis=1) if len(columns) > 1 else columns[0])
    stacked = jnp.dot(
        left_ref[...], jnp.concatenate([high, low, high], axis=0),
        preferred_element_type=jnp.float32,
    )
    return [
        (stacked[:side, i * side : (i + 1) * side], stacked[side:, i * side : (i + 1) * side])
        for i in range(len(waves))
    ]


def cos_sin(angle):
    turns = jnp.floor(angle * (2.0 / math.pi) + 0.5)
    rest = angle - turns * 1.5703125
    rest = rest - turns * 4.837512969970703e-4
    rest = rest - turns * 7.549789948768648e-8
    sq = rest * rest
    sin_part = rest + rest * sq * (-1.6666654611e-1 + sq * (8.3321608736e-3 + sq * -1.9515295891e-4))
    cos_part = 1.0 - 0.5 * sq + sq * sq * (
        4.166664568298827e-2 + sq * (-1.388731625493765e-3 + sq * 2.443315711809948e-5)
    )
    half = jnp.floor(turns * 0.5)
    odd = (turns - 2.0 * half) > 0.5
    flip = 1.0 - 2.0 * (half - 2.0 * jnp.floor(half * 0.5))
    cos_out = jnp.where(odd, -sin_part, cos_part) * flip
    sin_out = jnp.where(odd, cos_part, sin_part) * flip
    return cos_out, sin_out


def column_base(col, side, cols):
    return pl.multiple_of(jnp.minimum(col // side, cols // side - 2) * side, side)


def cut_kernel(above, index_ref, phase_ref, absorb_ref, out_ref, tall):
    windows, layers, _, side, _ = out_ref.shape
    cols = phase_ref.shape[2]
    for layer in range(layers):
        for which, source in enumerate((phase_ref, absorb_ref)):
            parts = [source[layer], jnp.zeros((side, cols), jnp.float32)]
            tall[layer, which, :side] = parts[above]
            tall[layer, which, side:] = parts[1 - above]

    def one(w, carried):
        row, col = index_ref[w], index_ref[windows + w]
        base = column_base(col, side, cols)
        shift = lax.rem(2 * side - (col - base), 2 * side)
        top = pl.multiple_of(row // 8 * 8, 8)
        lift = lax.rem(side + 8 - (row - top), side + 8)
        for layer in range(layers):
            for which in range(2):
                wide = tall[layer, which, pl.ds(top, side + 8), pl.ds(base, 2 * side)]
                narrow = pltpu.roll(wide, shift, 1)[:, :side]
                out_ref[w, layer, which] = pltpu.roll(narrow, lift, 0)[:side]
        return carried

    lax.fori_loop(0, windows, one, 0)


def place_kernel(own_ref, above_ref, own_pieces, above_pieces, out_phase, out_absorb, tall):
    windows, layers, _, side, _ = own_pieces.shape
    cols = out_phase.shape[2]
    tall[...] = jnp.zeros_like(tall)

    def place(index_ref, pieces_ref, start, w):
        row, col = index_ref[w], index_ref[windows + w]
        base = column_base(col, side, cols)
        shift = col - base
        top = pl.multiple_of(row // 8 * 8, 8)
        for layer in range(layers):
            for which in range(2):
                piece = pieces_ref[w, layer, which]
                long = pltpu.roll(jnp.concatenate([piece, jnp.zeros_like(piece[:8])], axis=0), row - top, 0)
                wide = pltpu.roll(jnp.concatenate([long, jnp.zeros_like(long)], axis=1), shift, 1)
                where = (layer, which, pl.ds(start + top, side + 8), pl.ds(base, 2 * side))
                tall[where] = tall[where] + wide

    @pl.loop(0, windows)
    def _(w):
        place(own_ref, own_pieces, side, w)

        @pl.when(lax.axis_index("tile") > 0)
        def _():
            place(above_ref, above_pieces, 0, w)

    for layer in range(layers):
        out_phase[layer] = tall[layer, 0, side : 2 * side]
        out_absorb[layer] = tall[layer, 1, side : 2 * side]


def greet():
    slab, slabs = lax.axis_index("slab"), lax.axis_size("slab")
    tile, tiles = lax.axis_index("tile"), lax.axis_size("tile")
    barrier = pltpu.get_barrier_semaphore()
    for step in range(1, slabs):
        pl.semaphore_signal(
            barrier, inc=1, device_id={"slab": lax.rem(slab + step, slabs)}, device_id_type=MESH
        )

    @pl.when(tile > 0)
    def _():
        pl.semaphore_signal(barrier, inc=1, device_id={"tile": tile - 1}, device_id_type=MESH)

    @pl.when(tile < tiles - 1)
    def _():
        pl.semaphore_signal(barrier, inc=1, device_id={"tile": tile + 1}, device_id_type=MESH)

    beside = (tile > 0).astype(jnp.int32) + (tile < tiles - 1).astype(jnp.int32)
    pl.semaphore_wait(barrier, slabs - 1 + beside)


def slot_plan(windows, slabs):
    moved = windows // 2
    kept = windows - moved
    homes = [(k % slabs, k // slabs) for k in range(windows + moved)]
    if windows % slabs == 0 and 0 < moved <= slabs:
        homes[windows:] = [(j * (slabs // moved), windows // slabs) for j in range(moved)]
    return kept, moved, homes, 1 + max(home[1] for home in homes)


def gather_kernel(
    own, above, measured, patches, measured_above,
    from_below, from_above, merged, zs_sem, zr_sem, xs_sem, xr_sem, ms_sem, mr_sem,
):
    windows, layers = own.shape[:2]
    slab, slabs = lax.axis_index("slab"), lax.axis_size("slab")
    tile, tiles = lax.axis_index("tile"), lax.axis_size("tile")
    kept, moved, homes, _ = slot_plan(windows, slabs)
    first, last = tile == 0, tile == tiles - 1
    greet()

    def up(i, l):
        return pltpu.make_async_remote_copy(
            src_ref=above.at[i, l], dst_ref=from_below.at[i, l], send_sem=zs_sem.at[i, l],
            recv_sem=zr_sem.at[i, l], device_id={"tile": tile - 1}, device_id_type=MESH)

    def down(j, l):
        return pltpu.make_async_remote_copy(
            src_ref=own.at[kept + j, l], dst_ref=from_above.at[j, l], send_sem=zs_sem.at[kept + j, l],
            recv_sem=zr_sem.at[kept + j, l], device_id={"tile": tile + 1}, device_id_type=MESH)

    def data_down(j):
        return pltpu.make_async_remote_copy(
            src_ref=measured.at[kept + j], dst_ref=measured_above.at[j], send_sem=ms_sem.at[j],
            recv_sem=mr_sem.at[j], device_id={"tile": tile + 1}, device_id_type=MESH)

    def across(k, source, l, sender):
        return pltpu.make_async_remote_copy(
            src_ref=source, dst_ref=patches.at[homes[k][1], sender * layers + l], send_sem=xs_sem.at[k, l],
            recv_sem=xr_sem.at[homes[k][1], sender, l], device_id={"slab": homes[k][0]}, device_id_type=MESH)

    @pl.loop(0, layers)
    def _(l):
        @pl.when(jnp.logical_not(first))
        def _():
            for i in range(kept):
                up(i, l).start()

        @pl.when(jnp.logical_not(last))
        def _():
            for j in range(moved):
                down(j, l).start()

    for j in range(moved):
        @pl.when(jnp.logical_not(last) & (slab == homes[kept + j][0]))
        def _():
            data_down(j).start()

    def hand_over(k, source, l):
        @pl.when(slab != homes[k][0])
        def _():
            across(k, source, l, slab).start()

        @pl.when(slab == homes[k][0])
        def _():
            patches[homes[k][1], slab * layers + l] = source[...]

    @pl.when(last)
    def _():
        @pl.loop(0, layers)
        def _(l):
            for j in range(moved):
                hand_over(windows + j, own.at[kept + j, l], l)

    @pl.loop(0, layers)
    def _(l):
        for i in range(kept):
            @pl.when(last)
            def _():
                merged[i, l] = own[i, l]

            @pl.when(jnp.logical_not(last))
            def _():
                up(i, l).wait_recv()
                merged[i, l] = own[i, l] + from_below[i, l]

            hand_over(i, merged.at[i, l], l)

        @pl.when(jnp.logical_not(first))
        def _():
            for j in range(moved):
                down(j, l).wait_recv()
                merged[kept + j, l] = above[kept + j, l] + from_above[j, l]
                hand_over(kept + j, merged.at[kept + j, l], l)

    for j in range(moved):
        @pl.when(jnp.logical_not(last) & (slab == homes[kept + j][0]))
        def _():
            data_down(j).wait_send()

        @pl.when(jnp.logical_not(first) & (slab == homes[kept + j][0]))
        def _():
            data_down(j).wait_recv()

    def finish(k, source):
        @pl.when(slab != homes[k][0])
        def _():
            @pl.loop(0, layers)
            def _(l):
                across(k, source.at[l], l, slab).wait_send()

        @pl.when(slab == homes[k][0])
        def _():
            for sender in range(slabs):
                @pl.when(sender != slab)
                def _():
                    @pl.loop(0, layers)
                    def _(l):
                        across(k, source.at[l], l, sender).wait_recv()

    for i in range(kept):
        finish(i, merged.at[i])

    @pl.when(jnp.logical_not(first))
    def _():
        for j in range(moved):
            finish(kept + j, merged.at[kept + j])

        @pl.loop(0, layers)
        def _(l):
            for i in range(kept):
                up(i, l).wait_send()

    @pl.when(last)
    def _():
        for j in range(moved):
            finish(windows + j, own.at[kept + j])

    @pl.when(jnp.logical_not(last))
    def _():
        @pl.loop(0, layers)
        def _(l):
            for j in range(moved):
                down(j, l).wait_send()


def wave_kernel(
    own_ref, above_ref, patches, probe_ref, measured_ref, above_measured_ref,
    q_left, q_right, qa_left, qa_right, f_left, f_right, fa_left, fa_right,
    own, above, grads, trans, mixed, zs_sem, xs_sem, own_sem, above_sem,
):
    depth, total, _, side, _ = patches.shape
    windows = measured_ref.shape[0]
    slab, slabs = lax.axis_index("slab"), lax.axis_size("slab")
    tile, tiles = lax.axis_index("tile"), lax.axis_size("tile")
    kept, moved, homes, _ = slot_plan(windows, slabs)

    layers = own.shape[1]
    first, last = tile == 0, tile == tiles - 1
    greet()

    def home(k, l):
        if k < kept:
            return own.at[k, l], own_sem.at[k, l]
        if k < windows:
            return above.at[k, l], above_sem.at[k, l]
        return own.at[k - moved, l], own_sem.at[k - moved, l]

    def across(k, l, target):
        place, sem = home(k, l)
        return pltpu.make_async_remote_copy(
            src_ref=grads.at[homes[k][1], target * layers + l], dst_ref=place,
            send_sem=xs_sem.at[homes[k][1], target, l], recv_sem=sem,
            device_id={"slab": target}, device_id_type=MESH)

    def down(i, l):
        return pltpu.make_async_remote_copy(
            src_ref=own.at[i, l], dst_ref=above.at[i, l], send_sem=zs_sem.at[i, l],
            recv_sem=above_sem.at[i, l], device_id={"tile": tile + 1}, device_id_type=MESH)

    def up(k, l):
        return pltpu.make_async_remote_copy(
            src_ref=above.at[k, l], dst_ref=own.at[k, l], send_sem=zs_sem.at[k, l],
            recv_sem=own_sem.at[k, l], device_id={"tile": tile - 1}, device_id_type=MESH)

    def give(k, s):
        target, l = s // layers, lax.rem(s, layers)

        @pl.when(slab != target)
        def _():
            across(k, l, target).start()

        @pl.when(slab == target)
        def _():
            home(k, l)[0][...] = grads[homes[k][1], s]

    def in_use(k):
        here = slab == homes[k][0]
        if k < kept:
            return here
        return here & (jnp.logical_not(first) if k < windows else last)

    def slot_at(d):
        slot = jnp.int32(-1)
        for k, (home_slab, home_depth) in enumerate(homes):
            if home_depth == d:
                slot = jnp.where(slab == home_slab, k, slot)
        return slot

    def valid(d):
        k = slot_at(d)
        mine = (k >= 0) & (k < kept)
        from_above = (k >= kept) & (k < windows) & (tile > 0)
        extra = (k >= windows) & (tile == tiles - 1)
        return mine | from_above | extra

    def excess_wave(d, wave):
        k = slot_at(d)
        is_above = (k >= kept) & (k < windows)
        own_at = jnp.clip(jnp.where(k < windows, k, k - moved), 0, windows - 1)
        above_at = jnp.clip(k, kept, windows - 1)
        live = jnp.where(is_above, above_ref[2 * windows + above_at], own_ref[2 * windows + own_at])
        target = jnp.where(is_above, above_measured_ref[above_at - kept], measured_ref[own_at])
        far_real, far_imag = wave
        excess = (0.5 * live.astype(jnp.float32)) * (far_real * far_real + far_imag * far_imag - target)
        return excess * far_real, excess * far_imag

    def run(slots):
        def prepare(s):
            for d in slots:
                damping = jnp.exp(-patches[d, s, 1])
                cos_part, sin_part = cos_sin(patches[d, s, 0])
                trans[d, s, 0] = damping * cos_part
                trans[d, s, 1] = damping * sin_part

        prepare(0)

        def forward(s, waves):
            entering = []
            for d, (wave_real, wave_imag) in zip(slots, waves):
                t_real, t_imag = trans[d, s, 0], trans[d, s, 1]
                mixed_real = t_real * wave_real - t_imag * wave_imag
                mixed_imag = t_real * wave_imag + t_imag * wave_real
                mixed[d, s, 0] = mixed_real
                mixed[d, s, 1] = mixed_imag
                entering.append((mixed_real, mixed_imag))
            leaving = sandwich(q_left, q_right, entering)
            prepare(jnp.minimum(s + 1, total - 1))
            return tuple(leaving)

        waves = lax.fori_loop(0, total, forward, tuple((probe_ref[0], probe_ref[1]) for d in slots))
        far = sandwich(f_left, f_right, waves)
        seeds = [excess_wave(d, wave) for d, wave in zip(slots, far)]
        backs = tuple(sandwich(fa_left, fa_right, seeds))

        def backward(i, backs):
            s = total - 1 - i
            result = []
            for d, (m_real, m_imag) in zip(slots, sandwich(qa_left, qa_right, backs)):
                u_real, u_imag = mixed[d, s, 0], mixed[d, s, 1]
                t_real, t_imag = trans[d, s, 0], trans[d, s, 1]
                grads[d, s, 0] = u_real * m_imag - u_imag * m_real
                grads[d, s, 1] = -(u_real * m_real + u_imag * m_imag)
                result.append((t_real * m_real + t_imag * m_imag, t_real * m_imag - t_imag * m_real))
            for k, (_, home_depth) in enumerate(homes):
                if home_depth in slots:
                    @pl.when(in_use(k))
                    def _():
                        give(k, s)

            return tuple(result)

        lax.fori_loop(0, total, backward, backs)

    deeper = valid(1) if depth > 1 else jnp.bool_(False)

    @pl.when(valid(0) & jnp.logical_not(deeper))
    def _():
        run([0])

    if depth > 1:
        @pl.when(deeper)
        def _():
            run(list(range(depth)))

    def arrive(k, l):
        @pl.when(slab != homes[k][0])
        def _():
            across(k, l, slab).wait_recv()

    @pl.loop(0, layers)
    def _(back):
        l = layers - 1 - back
        for k in range(kept):
            arrive(k, l)

            @pl.when(jnp.logical_not(last))
            def _():
                down(k, l).start()

        @pl.when(jnp.logical_not(first))
        def _():
            for k in range(kept, windows):
                arrive(k, l)
                up(k, l).start()

    def sent(k, l):
        @pl.when(slab == homes[k][0])
        def _():
            for target in range(slabs):
                @pl.when(slab != target)
                def _():
                    across(k, l, target).wait_send()

    @pl.loop(0, layers)
    def _(l):
        for k in range(kept):
            sent(k, l)

        @pl.when(jnp.logical_not(first))
        def _():
            for k in range(kept, windows):
                sent(k, l)
                up(k, l).wait_send()
            for k in range(kept):
                down(k, l).wait_recv()

        @pl.when(jnp.logical_not(last))
        def _():
            for k in range(kept):
                down(k, l).wait_send()
            for k in range(kept, windows):
                up(k, l).wait_recv()

        @pl.when(last)
        def _():
            for k in range(windows, windows + moved):
                arrive(k, l)
                sent(k, l)


def passed_along(array, axis, by):
    devices = lax.axis_size(axis)
    pairs = [(i, i + by) for i in range(devices) if 0 <= i + by < devices]
    return lax.ppermute(array, axis, pairs)


def params(**more):
    return pltpu.CompilerParams(vmem_limit_bytes=vmem_limit, **more)


def local(phase_map, absorption, probe_wave, measured, rows_at, cols_at, live_mask):
    layers, rows, cols = phase_map.shape
    side = probe_wave.shape[2]
    windows = measured.shape[0]
    slabs = lax.axis_size("slab")
    kept, moved, homes, depth = slot_plan(windows, slabs)
    smem = pl.BlockSpec(memory_space=pltpu.SMEM)
    vmem = pl.BlockSpec(memory_space=pltpu.VMEM)
    f32 = jnp.float32
    dma = pltpu.SemaphoreType.DMA
    pieces = jax.ShapeDtypeStruct((windows, layers, 2, side, side), f32)
    stacked = jax.ShapeDtypeStruct((depth, slabs * layers, 2, side, side), f32)

    index_own = jnp.concatenate([rows_at, cols_at, live_mask])
    index_above = passed_along(index_own, "tile", 1)
    own, above = (
        pl.pallas_call(
            functools.partial(cut_kernel, which),
            out_shape=pieces,
            in_specs=[smem, vmem, vmem],
            out_specs=vmem,
            scratch_shapes=[pltpu.VMEM((layers, 2, 2 * side, cols), f32)],
            compiler_params=params(),
            cost_estimate=pl.CostEstimate(
                flops=0, bytes_accessed=8 * layers * side * (cols + windows * side), transcendentals=0
            ),
            name=name,
        )(index, phase_map, absorption)
        for which, name, index in ((0, "cut_own", index_own), (1, "cut_above", index_above))
    )
    patches, measured_above = pl.pallas_call(
        gather_kernel,
        out_shape=(stacked, jax.ShapeDtypeStruct((moved, side, side), f32)),
        in_specs=[vmem, vmem, vmem],
        out_specs=(vmem, vmem),
        scratch_shapes=[
            pltpu.VMEM((kept,) + pieces.shape[1:], f32),
            pltpu.VMEM((moved,) + pieces.shape[1:], f32),
            pltpu.VMEM(pieces.shape, f32),
            dma((windows, layers)),
            dma((windows, layers)),
            dma((windows + moved, layers)),
            dma((depth, slabs, layers)),
            dma((moved,)),
            dma((moved,)),
        ],
        compiler_params=params(collective_id=0, has_side_effects=True),
        name="gather",
    )(own, above, measured)

    mats = [jnp.asarray(m) for m in tables(side)]
    own, above = pl.pallas_call(
        wave_kernel,
        out_shape=(pieces, pieces),
        in_specs=[smem, smem] + [vmem] * (4 + len(mats)),
        out_specs=(vmem, vmem),
        scratch_shapes=[
            pltpu.VMEM(stacked.shape, f32),
            pltpu.VMEM(stacked.shape, f32),
            pltpu.VMEM(stacked.shape, f32),
            dma((windows, layers)),
            dma((depth, slabs, layers)),
            dma((windows, layers)),
            dma((windows, layers)),
        ],
        compiler_params=params(collective_id=1, has_side_effects=True),
        name="waves",
    )(index_own, index_above, patches, probe_wave, measured, measured_above, *mats)
    whole = jax.ShapeDtypeStruct(phase_map.shape, f32)
    return pl.pallas_call(
        place_kernel,
        out_shape=(whole, whole),
        in_specs=[smem, smem, vmem, vmem],
        out_specs=(vmem, vmem),
        scratch_shapes=[pltpu.VMEM((layers, 2, 3 * side, cols), f32)],
        compiler_params=params(),
        name="place",
    )(index_own, index_above, own, above)


def solution(mesh):
    return jax.shard_map(
        local,
        mesh=mesh,
        in_specs=(
            P(("groups", "slab"), "tile", None),
            P(("groups", "slab"), "tile", None),
            P(),
            P(("groups", "tile"), None, None),
            P(("groups", "tile")),
            P(("groups", "tile")),
            P(("groups", "tile")),
        ),
        out_specs=(P(("groups", "slab"), "tile", None), P(("groups", "slab"), "tile", None)),
        check_vma=False,
    )
```
